256 devices in a mesh: outer: 32 (over z, y), inner: 8 (over x, core).
Axes of the slice: x: 4, y: 4, z: 8, core: 2. Of those that a mesh axis runs over, the one named last changes fastest.
Arguments:
- based_query: bfloat16 [32768, 110], P(('outer', 'inner')), may hold values from -5 to 5
- based_key: bfloat16 [32768, 110], P(('outer', 'inner')), may hold values from -5 to 5
- based_value: bfloat16 [32768, 640], P(('outer', 'inner')), may hold values from -6 to 6
- norm_gain: float32 [640], replicated, may hold values from 0.1 to 1.9
- doc_ids: int32 [32768], P(('outer', 'inner')), may hold values from 0 to 15, never falling along the last dimension, each value on 1 to 8192 neighbouring positions
- window_query: bfloat16 [32768, 1280], P(('outer', 'inner')), may hold values from -4.5 to 4.5
- window_key: bfloat16 [32768, 1280], P(('outer', 'inner')), may hold values from -4.5 to 4.5
- window_value: bfloat16 [32768, 1280], P(('outer', 'inner')), may hold values from -6 to 6
Outputs:
- based_out: bfloat16 [32768, 640], P(('outer', 'inner'))
- window_out: bfloat16 [32768, 1280], P(('outer', 'inner'))
The draws below stay inside these ranges and needn't reach their ends.
All inputs are finite; a program needn't handle non-finite values.
Results may differ from the reference program's by a relative error of at most 0.004.
Values may be sent and summed in bfloat16 or wider, within the bound.
A program may use at most 320 MiB of HBM per device.

```python
import math
import jax
import jax.numpy as jnp
import numpy as np
from jax import lax

HEADS = 10
BASED_DIM = 64
HEAD_DIM = 128
QK_DIM = 11
WIN_HEADS = 10
WINDOW = 1024
DOCS = 16
TOK_DEV = 128
FEATURES = 144
TOKENS = 32768


def window_pair(key):
    width = WIN_HEADS * HEAD_DIM
    first, second = jax.random.split(key, 2)
    query = jnp.clip(jax.random.normal(first, (TOKENS, width), jnp.float32), -4.5, 4.5)
    keys = jnp.clip(jax.random.normal(second, (TOKENS, width), jnp.float32), -4.5, 4.5)
    return (query, keys)


def draw_window_query(key, part):
    query, keys = window_pair(jax.random.fold_in(key, 11))
    return query.astype(jnp.bfloat16)


def draw_window_key(key, part):
    query, keys = window_pair(jax.random.fold_in(key, 11))
    return keys.astype(jnp.bfloat16)


def levels(stream_key, shape, shards, low, top_value):
    level, own = 1.0, jax.random.fold_in(stream_key, 6)
    for axis_at, parts in shards:
        draws = jnp.exp(jax.random.uniform(jax.random.fold_in(own, axis_at), (parts,), jnp.float32, low / len(shards), top_value / len(shards)))
        level = level * jnp.repeat(draws, shape[axis_at] // parts).reshape([-1 if axis == axis_at else 1 for axis in range(len(shape))])
    return level


def profile(amount, total, limit, skew):
    loads = [(1 << 20) // math.isqrt(grade ** skew) + 1 for grade in range(2, amount + 1)]
    rest, given = total - limit - (amount - 1), [1] * (amount - 1)
    while rest > 0:
        free = [i for i in range(amount - 1) if given[i] < limit]
        whole, budget = sum([loads[i] for i in free]), rest
        for i in free:
            more = min(limit - given[i], max(1, budget * loads[i] // whole), rest)
            given[i] = given[i] + more
            rest = rest - more
    return np.array([limit] + given)


def uneven(stream_key, number_of, total, bound, slope):
    if number_of == 2:
        one = jax.random.randint(stream_key, (), max(1, total - bound), min(bound, total - 1) + 1)
        return jnp.stack([one, total - one])
    sizes = jnp.asarray(profile(number_of, total, bound, slope), jnp.int32)
    couples = (number_of - 1) // 2
    donor, sink = sizes[1:1 + 2 * couples:2], sizes[2:2 + 2 * couples:2]
    slack = jnp.minimum(donor - 1, bound - sink)
    shifted = jax.random.randint(jax.random.fold_in(stream_key, 1), (couples,), 0, 1 << 20) % (slack + 1)
    sizes = sizes.at[1:1 + 2 * couples:2].set(donor - shifted).at[2:2 + 2 * couples:2].set(sink + shifted)
    return sizes[jax.random.permutation(jax.random.fold_in(stream_key, 2), number_of)]


def noise(stream_key, extent, spread, limit, pieces=(), kind=jnp.bfloat16):
    level = levels(stream_key, extent, pieces, -0.22, 0.18) if pieces else 1.0
    result = jax.random.normal(stream_key, extent, jnp.float32) * spread * level
    return jnp.minimum(jnp.maximum(result, -limit), limit).astype(kind)


def setup_inputs(seed: int = 0) -> dict:
    streams_of = jax.random.split(jax.random.key(seed), 9)
    based_query = noise(streams_of[0], (TOKENS, HEADS * QK_DIM), 1.0, 5.0, ((0, 256),))
    based_key = noise(streams_of[1], (TOKENS, HEADS * QK_DIM), 1.0, 5.0, ((0, 256),))
    based_value = noise(streams_of[2], (TOKENS, HEADS * BASED_DIM), 1.0, 6.0, ((0, 256),))
    norm_gain = jnp.clip(1.0 + 0.18 * jax.random.normal(streams_of[3], (HEADS * BASED_DIM,), jnp.float32), 0.1, 1.9)
    doc_ids = jnp.searchsorted(jnp.cumsum(uneven(streams_of[4], DOCS, TOKENS, TOKENS // 4, 0)), jnp.arange(TOKENS), side="right").astype(jnp.int32)
    window_query = draw_window_query(jax.random.fold_in(streams_of[8], 71), 0)
    window_key = draw_window_key(jax.random.fold_in(streams_of[8], 71), 0)
    window_value = noise(streams_of[7], (TOKENS, WIN_HEADS * HEAD_DIM), 1.0, 6.0, ((0, 256),))
    return dict(based_query=based_query, based_key=based_key, based_value=based_value, norm_gain=norm_gain, doc_ids=doc_ids, window_query=window_query, window_key=window_key, window_value=window_value)


def lift_rows(proj):
    rows = proj.shape[0]
    half = proj.astype(jnp.float32).reshape(rows, HEADS, QK_DIM) * 0.5
    ones = jnp.ones((rows, HEADS, 1), jnp.float32)
    return jnp.concatenate([ones, half], axis=2)

def feature_map(lifted):
    rows = lifted.shape[0]
    outer = lifted[:, :, :, None] * lifted[:, :, None, :]
    return outer.reshape(rows, HEADS, FEATURES).astype(jnp.bfloat16)

def based_block(carry, block):
    state, carry_doc = carry
    query, key_in, value, docs, gain = (block[0], block[1], block[2], block[3], block[4])
    rows = query.shape[0]
    lifted_q = lift_rows(query)
    lifted_k = lift_rows(key_in)
    feat_q = feature_map(lifted_q)
    feat_k = feature_map(lifted_k)
    values = value.reshape(rows, HEADS, BASED_DIM).astype(jnp.float32)
    inter = jnp.einsum('thf,hfd->thd', feat_q.astype(jnp.float32), state, precision=lax.Precision.HIGHEST)
    inter = inter * (docs == carry_doc).astype(jnp.float32)[:, None, None]
    kernel = jnp.einsum('ihp,jhp->hij', lifted_q, lifted_k, precision=lax.Precision.HIGHEST) ** 2
    place = jnp.arange(rows, dtype=jnp.int32)
    visible = (place[None, :] <= place[:, None]) & (docs[None, :] == docs[:, None])
    weights = jnp.where(visible[None], kernel, 0.0).astype(jnp.bfloat16)
    intra = jnp.einsum('hij,jhd->ihd', weights.astype(jnp.float32), values, precision=lax.Precision.HIGHEST)
    total = inter + intra
    normed = total * lax.rsqrt(lax.optimization_barrier(jnp.mean(total * total, axis=2, keepdims=True)) + 1e-05)
    output = (normed.reshape(rows, HEADS * BASED_DIM) * gain).astype(jnp.bfloat16)
    last_doc = docs[rows - 1]
    keep = (docs == last_doc).astype(jnp.float32)
    local = jnp.einsum('thf,thd->hfd', feat_k.astype(jnp.float32) * keep[:, None, None], values, precision=lax.Precision.HIGHEST)
    state = jnp.where(last_doc == carry_doc, state, 0.0) + local
    return ((state, last_doc), output)

def reference(based_query, based_key, based_value, norm_gain, doc_ids, window_query, window_key, window_value):
    blocks = TOKENS // TOK_DEV
    gain = norm_gain.astype(jnp.float32)

    def step(carry, items):
        return based_block(carry, (items[0], items[1], items[2], items[3], gain))
    init = (jnp.zeros((HEADS, FEATURES, BASED_DIM), jnp.float32), jnp.int32(-1))
    items = (based_query.reshape(blocks, TOK_DEV, HEADS * QK_DIM), based_key.reshape(blocks, TOK_DEV, HEADS * QK_DIM), based_value.reshape(blocks, TOK_DEV, HEADS * BASED_DIM), doc_ids.reshape(blocks, TOK_DEV))
    final, based_parts = lax.scan(step, init, items)
    based_out = based_parts.reshape(TOKENS, HEADS * BASED_DIM)
    width = WIN_HEADS * HEAD_DIM
    key_pad = jnp.concatenate([jnp.zeros((WINDOW, width), jnp.bfloat16), window_key], axis=0)
    value_pad = jnp.concatenate([jnp.zeros((WINDOW, width), jnp.bfloat16), window_value], axis=0)
    doc_pad = jnp.concatenate([jnp.full((WINDOW,), -1, jnp.int32), doc_ids], axis=0)
    scale = 1.0 / math.sqrt(HEAD_DIM)

    def window_block(index):
        base = (index * TOK_DEV).astype(jnp.int32)
        query = lax.dynamic_slice_in_dim(window_query, base, TOK_DEV, 0).astype(jnp.float32).reshape(TOK_DEV, WIN_HEADS, HEAD_DIM)
        keys = lax.dynamic_slice_in_dim(key_pad, base, TOK_DEV + WINDOW, 0).astype(jnp.float32).reshape(TOK_DEV + WINDOW, WIN_HEADS, HEAD_DIM)
        vals = lax.dynamic_slice_in_dim(value_pad, base, TOK_DEV + WINDOW, 0).astype(jnp.float32).reshape(TOK_DEV + WINDOW, WIN_HEADS, HEAD_DIM)
        docs_q = lax.dynamic_slice_in_dim(doc_ids, base, TOK_DEV, 0)
        docs_k = lax.dynamic_slice_in_dim(doc_pad, base, TOK_DEV + WINDOW, 0)
        row_place = jnp.arange(TOK_DEV, dtype=jnp.int32)
        col_place = jnp.arange(TOK_DEV + WINDOW, dtype=jnp.int32)
        visible = (col_place[None, :] > row_place[:, None]) & (col_place[None, :] <= row_place[:, None] + WINDOW) & (docs_k[None, :] == docs_q[:, None])
        scores = jnp.einsum('ahd,bhd->hab', query, keys, precision=lax.Precision.HIGHEST) * scale
        scores = jnp.where(visible[None], scores, -1e+30)
        top = lax.optimization_barrier(jnp.max(scores, axis=2, keepdims=True))
        probs = jnp.exp(scores - top)
        rowsum = lax.optimization_barrier(jnp.sum(probs, axis=2, keepdims=True))
        mixed = jnp.einsum('hab,bhd->had', probs.astype(jnp.bfloat16).astype(jnp.float32), vals, precision=lax.Precision.HIGHEST) / rowsum
        return mixed.astype(jnp.bfloat16).transpose(1, 0, 2).reshape(TOK_DEV, width)
    window_parts = lax.map(window_block, jnp.arange(blocks, dtype=jnp.int32))
    window_out = window_parts.reshape(TOKENS, width)
    return (based_out, window_out)
```

```python
import functools
import math

import jax
import jax.numpy as jnp
import numpy as np
from jax import lax
from jax.experimental import pallas as pl
from jax.experimental.pallas import tpu as pltpu
from jax.sharding import PartitionSpec as P

HEADS = 10
BASED_DIM = 64
HEAD_DIM = 128
QK_DIM = 11
WIN_HEADS = 10
ROWS = 128
BACK = 8
FEAT = 80
PAIRS = HEADS // 2
SLICE = 64
MESH = pl.DeviceIdType.MESH
ORDER = ((0, 1), (1, 0), (1, 1), (3, 0), (3, 1), (2, 0), (2, 1))
NT = (((1,), (1,)), ((), ()))
TN = (((0,), (0,)), ((), ()))
F32 = jnp.float32
BF16 = jnp.bfloat16


def feature_table():
    table = np.zeros((8, HEADS * 128), np.float32)
    table[:2] = -1.0
    for head in range(HEADS):
        at = head * 128
        for a in range(QK_DIM + 1):
            for b in range(a, QK_DIM + 1):
                for row, entry in ((0, a), (1, b)):
                    if entry == 0:
                        table[row + 2, at] = 1.0
                    else:
                        table[row, at] = head * QK_DIM + entry - 1
                table[4, at] = 1.0 if a == b else 2.0
                at += 1
    return table


def kernel(
    outer,
    bq, bk, bv, gain, doc, aux, wq, wk, wv,
    bout, wout,
    kv, cfw, qb, ob, dsl, dk, d2, ssend, srecv, tsend, trecv, fsend, pf, tot, phq,
    rs_own, ss_own, rs_prev, ss_prev, rs_q, ss_q, rs_o, ss_o, rs_c, ss_c,
    rs_d, ss_d, rs_dk, ss_dk, rs_s, ss_s, rs_t, ss_t, rs_f, ss_f,
):
    r = lax.axis_index("outer")
    i = lax.axis_index("inner")
    x = i // 2
    c = i % 2
    up = lax.rem(r + 1, outer)

    def to(dx, dc):
        return lax.rem(x + dx, 4) * 2 + lax.rem(c + dc, 2)

    def frm(dx, dc):
        return lax.rem(x + 4 - dx, 4) * 2 + lax.rem(c + dc, 2)

    def cols(ref, head):
        return ref.at[:, pl.ds(pl.multiple_of(head * HEAD_DIM, HEAD_DIM), HEAD_DIM)]

    def remote(src, dst, ss, rs, row, inner):
        return pltpu.make_async_remote_copy(
            src_ref=src, dst_ref=dst, send_sem=ss, recv_sem=rs,
            device_id=(row, inner), device_id_type=MESH,
        )

    def arrived(dst, rs):
        pltpu.make_async_copy(dst, dst, rs).wait()

    sent = []

    def send(src, dst, ss, rs, row, inner):
        copy = remote(src, dst, ss, rs, row, inner)
        copy.start()
        sent.append((src, ss))

    doc_row = doc[...].astype(F32)
    dsl[i] = jnp.broadcast_to(doc_row, (8, 128))

    barrier = pltpu.get_barrier_semaphore()
    for dx, dc in ORDER:
        pl.semaphore_signal(barrier, inc=1, device_id=(r, to(dx, dc)), device_id_type=MESH)
    for k in range(1, BACK + 1):
        pl.semaphore_signal(
            barrier, inc=1, device_id=(lax.rem(r + outer - k, outer), i), device_id_type=MESH
        )
    pl.semaphore_wait(barrier, len(ORDER) + BACK)

    for h in range(2):
        for part, ref in ((0, wk), (1, wv)):
            send(cols(ref, 8 + h), cfw.at[h, part], ss_c.at[h, part], rs_c.at[h, part], up, i)
    for part, ref in ((0, wk), (1, wv)):
        pltpu.make_async_copy(cols(ref, i), kv.at[0, 8 + i, part], rs_own.at[0, i, part]).start()
        pltpu.make_async_copy(cols(ref, 8 + c), kv.at[1, 8 + i, part], rs_own.at[1, i, part]).start()
    pltpu.make_async_copy(cols(wq, i), qb.at[i], rs_q.at[i]).start()
    pltpu.make_async_copy(cols(wq, 8 + c), qb.at[8 + c], rs_q.at[8 + c]).start()
    for n, (dx, dc) in enumerate(ORDER):
        d = to(dx, dc)
        send(dsl.at[i], dsl.at[i], ss_d.at[n], rs_d.at[i], r, d)
    for n, (dx, dc) in enumerate(ORDER):
        d = to(dx, dc)
        for part, ref in ((0, wk), (1, wv)):
            send(
                cols(ref, d), kv.at[0, 8 + i, part], ss_own.at[0, n, part],
                rs_own.at[0, i, part], r, d,
            )
    sib = x * 2 + (1 - c)
    for part, ref in ((0, wk), (1, wv)):
        send(
            cols(ref, 9 - c), kv.at[1, 8 + i, part], ss_own.at[1, 0, part],
            rs_own.at[1, i, part], r, sib,
        )
    send(cols(wq, 9 - c), qb.at[8 + c], ss_q.at[7], rs_q.at[8 + c], r, sib)

    for part in range(2):
        arrived(kv.at[0, 8 + i, part], rs_own.at[0, i, part])
    send(kv.at[0, 8 + i], kv.at[0, i], ss_prev.at[0, i], rs_prev.at[0, i], up, i)

    table = aux[...]
    lane110 = lax.broadcasted_iota(jnp.int32, (QK_DIM * HEADS, HEADS * 128), 0).astype(F32)
    pick_a = jnp.where(lane110 == table[0:1, :], 0.5, 0.0).astype(BF16)
    pick_b = jnp.where(lane110 == table[1:2, :], 0.5, 0.0).astype(BF16)
    xq = bq[...]
    xk = bk[...]

    def features(proj):
        first = jnp.dot(proj, pick_a, preferred_element_type=F32) + table[2:3, :]
        second = jnp.dot(proj, pick_b, preferred_element_type=F32) + table[3:4, :]
        return first * second

    lane = lax.broadcasted_iota(jnp.int32, (128, 128), 1)
    row = lax.broadcasted_iota(jnp.int32, (128, 128), 0)
    own_rows = jnp.broadcast_to(doc_row, (128, 128))
    own_cols = own_rows.T
    keep = own_cols == doc_row[:, 127:128]
    fk = features(xk).astype(BF16)
    left80 = lax.broadcasted_iota(jnp.int32, (128, 128), 1) < BASED_DIM
    for p in range(PAIRS):
        vals = bv[:, p * 128 : (p + 1) * 128]
        kept = jnp.where(keep, vals.astype(F32), 0.0).astype(BF16)
        both = [
            lax.dot_general(
                fk[:, h * 128 : (h + 1) * 128], kept, TN, preferred_element_type=F32
            )
            for h in (2 * p, 2 * p + 1)
        ]
        state = jnp.where(left80, both[0], both[1])
        ssend[p * FEAT : (p + 1) * FEAT, :] = state[:FEAT].astype(BF16)
    ssend[PAIRS * FEAT :, :] = jnp.zeros((8 * SLICE - PAIRS * FEAT, 128), BF16)

    def block(ref, d):
        return ref.at[pl.ds(pl.multiple_of(d * SLICE, SLICE), SLICE)]

    pltpu.make_async_copy(block(ssend, i), srecv.at[i], rs_s.at[i]).start()
    for n, (dx, dc) in enumerate(ORDER):
        d = to(dx, dc)
        send(block(ssend, d), srecv.at[i], ss_s.at[n], rs_s.at[i], r, d)

    for h in range(2):
        for part in range(2):
            arrived(cfw.at[h, part], rs_c.at[h, part])
    pltpu.make_async_copy(cfw.at[c], kv.at[1, i], rs_prev.at[1, i]).start()
    send(cfw.at[1 - c], kv.at[1, i], ss_prev.at[1, 0], rs_prev.at[1, i], r, sib)
    for dx in (1, 3, 2):
        for dc in range(2):
            n = dx * 2 + dc - 1
            h = lax.rem(c + dc, 2)
            d = to(dx, dc)

            @pl.when(x + dx < 4)
            def _():
                for part, ref in ((0, wk), (1, wv)):
                    remote(
                        cols(ref, 8 + h), kv.at[1, 8 + i, part], ss_own.at[1, n, part],
                        rs_own.at[1, i, part], r, d,
                    ).start()

            @pl.when(x + dx >= 4)
            def _():
                remote(
                    cfw.at[h], kv.at[1, i], ss_prev.at[1, n], rs_prev.at[1, i], r, d
                ).start()

    for n, (dx, dc) in enumerate(ORDER):
        s = frm(dx, dc)
        for part in range(2):
            arrived(kv.at[0, 8 + s, part], rs_own.at[0, s, part])
        send(kv.at[0, 8 + s], kv.at[0, s], ss_prev.at[0, s], rs_prev.at[0, s], up, i)
    for n, (dx, dc) in enumerate(ORDER):
        d = to(dx, dc)
        send(cols(wq, d), qb.at[i], ss_q.at[n], rs_q.at[i], r, d)

    for dx, dc in ORDER:
        s = frm(dx, dc)
        arrived(dsl.at[s], rs_d.at[s])
    sub = lax.broadcasted_iota(jnp.int32, (8, 128), 0)
    row_docs = jnp.zeros((8, 128), F32)
    for s in range(8):
        row_docs = jnp.where(sub == s, dsl[s], row_docs)
    dk[0] = row_docs
    for k in range(1, BACK + 1):
        send(dk.at[0], dk.at[k], ss_dk.at[k], rs_dk.at[k], lax.rem(r + k, outer), i)

    arrived(srecv.at[i], rs_s.at[i])
    for dx, dc in ORDER:
        s = frm(dx, dc)
        arrived(srecv.at[s], rs_s.at[s])
    last = [row_docs[s : s + 1, 127:128] for s in range(8)]
    acc = srecv[0].astype(F32)
    running = []
    for s in range(1, 8):
        running.append(acc)
        acc = srecv[s].astype(F32) + jnp.where(last[s] == last[s - 1], acc, 0.0)
    tsend[...] = acc
    for k in range(1, BACK + 1):
        send(tsend, trecv.at[k - 1], ss_t.at[k], rs_t.at[k], lax.rem(r + k, outer), i)

    inside = (own_cols == own_rows) & (lane <= row)
    lane_q = lax.broadcasted_iota(jnp.int32, (128, QK_DIM * HEADS), 1)
    for p in range(PAIRS):
        vals = bv[:, p * 128 : (p + 1) * 128]
        both = []
        for h in (2 * p, 2 * p + 1):
            mine = (lane_q >= h * QK_DIM) & (lane_q < (h + 1) * QK_DIM)
            part_q = jnp.where(mine, xq.astype(F32), 0.0).astype(BF16)
            dots = lax.dot_general(part_q, xk, NT, preferred_element_type=F32) * 0.25 + 1.0
            weight = jnp.where(inside, dots * dots, 0.0).astype(BF16)
            both.append(jnp.dot(weight, vals, preferred_element_type=F32))
        tot[p] = jnp.where(left80, both[0], both[1])
    phq[...] = (features(xq) * table[4:5, :]).astype(BF16)

    for k in range(1, BACK + 1):
        arrived(dk.at[k], rs_dk.at[k])
        arrived(trecv.at[k - 1], rs_t.at[k])
    entering_doc = jnp.where(r >= 1, dk[1][7:8, 127:128], -1.0)
    enter = jnp.zeros((SLICE, 128), F32)
    for k in range(1, BACK + 1):
        same = jnp.where(r >= k, dk[k][7:8, 127:128], -2.0) == entering_doc
        enter = enter + jnp.where(same, trecv[k - 1], 0.0)
    fsend[0] = enter.astype(BF16)
    for s in range(1, 8):
        fsend[s] = (running[s - 1] + jnp.where(last[s - 1] == entering_doc, enter, 0.0)).astype(BF16)
    pltpu.make_async_copy(fsend.at[i], block(pf, i), rs_f.at[i]).start()
    for n, (dx, dc) in enumerate(ORDER):
        d = to(dx, dc)
        send(fsend.at[d], block(pf, i), ss_f.at[n], rs_f.at[i], r, d)
    d2[0:8] = jnp.where(r >= 1, dk[1], -1.0)
    d2[8:16] = row_docs

    factor = math.log2(math.e) / math.sqrt(HEAD_DIM)

    def attend(b, j, at):
        query = qb[at]
        docq = jnp.broadcast_to(d2[pl.ds(8 + j, 1), :], (128, 128)).T
        scores = []
        top = None
        for t in range(BACK + 1):
            block_scores = lax.dot_general(
                query, kv[b, j + t, 0], NT, preferred_element_type=F32
            )
            see = docq == d2[pl.ds(j + t, 1), :]
            if t == 0:
                see = see & (lane > row)
            if t == BACK:
                see = see & (lane <= row)
            block_scores = jnp.where(see, block_scores, -1e30)
            scores.append(block_scores)
            top = block_scores if top is None else jnp.maximum(top, block_scores)
        peak = jnp.max(top, axis=1, keepdims=True)
        whole = None
        mixed = None
        for t in range(BACK + 1):
            prob = jnp.exp2((scores[t] - peak) * factor)
            whole = prob if whole is None else whole + prob
            term = jnp.dot(prob.astype(BF16), kv[b, j + t, 1], preferred_element_type=F32)
            mixed = term if mixed is None else mixed + term
        rowsum = jnp.sum(whole, axis=1, keepdims=True)
        ob[at] = (mixed / rowsum).astype(BF16)

    arrived(qb.at[8 + c], rs_q.at[8 + c])
    arrived(qb.at[9 - c], rs_q.at[9 - c])

    @pl.loop(0, 2 * x + 2)
    def _(s):
        for part in range(2):
            arrived(kv.at[1, 8 + s, part], rs_own.at[1, s, part])

    @pl.loop(2 * x, 8)
    def _(s):
        arrived(kv.at[1, s], rs_prev.at[1, s])

    @pl.loop(0, 2)
    def _(core):
        attend(1, 2 * x + core, 8 + core)

    send(ob.at[9 - c], cols(wout, 8 + c), ss_o.at[8], rs_o.at[8 + c], r, sib)
    pltpu.make_async_copy(ob.at[8 + c], cols(wout, 8 + c), ss_o.at[9]).start()

    @pl.loop(0, 8)
    def _(step):
        j = 7 - step

        arrived(qb.at[j], rs_q.at[j])
        arrived(kv.at[0, j], rs_prev.at[0, j])
        attend(0, j, j)

        @pl.when(j != i)
        def _():
            remote(ob.at[j], cols(wout, i), ss_o.at[j], rs_o.at[i], r, j).start()

        @pl.when(j == i)
        def _():
            pltpu.make_async_copy(ob.at[j], cols(wout, i), ss_o.at[j]).start()

    arrived(block(pf, i), rs_f.at[i])
    for dx, dc in ORDER:
        s = frm(dx, dc)
        arrived(block(pf, s), rs_f.at[s])
    previous = jnp.where(i == 0, entering_doc, -1.0)
    for s in range(1, 8):
        previous = jnp.where(i == s, last[s - 1], previous)
    carried = own_cols == previous
    rest = jnp.zeros((128 - FEAT, 128), BF16)
    for p in range(PAIRS):
        state = jnp.concatenate([pf[p * FEAT : (p + 1) * FEAT, :], rest], axis=0)
        both = [
            jnp.dot(phq[:, h * 128 : (h + 1) * 128], state, preferred_element_type=F32)
            for h in (2 * p, 2 * p + 1)
        ]
        total = tot[p] + jnp.where(carried, jnp.where(left80, both[0], both[1]), 0.0)
        square = total * total
        one = jnp.sum(jnp.where(left80, square, 0.0), axis=1, keepdims=True)
        two = jnp.sum(jnp.where(left80, 0.0, square), axis=1, keepdims=True)
        mean = jnp.where(left80, one, two) * (1.0 / BASED_DIM)
        scaled = total * lax.rsqrt(mean + 1e-5) * gain[:, p * 128 : (p + 1) * 128]
        bout[:, p * 128 : (p + 1) * 128] = scaled.astype(BF16)

    @pl.loop(0, 8)
    def _(j):
        @pl.when(j != i)
        def _():
            arrived(cols(wout, j), rs_o.at[j])

    arrived(cols(wout, 9 - c), rs_o.at[9 - c])
    for src, ss in sent:
        arrived(src, ss)
    for dx in (1, 3, 2):
        for dc in range(2):
            n = dx * 2 + dc - 1

            @pl.when(x + dx < 4)
            def _():
                for part in range(2):
                    arrived(kv.at[1, 8 + i, part], ss_own.at[1, n, part])

            @pl.when(x + dx >= 4)
            def _():
                arrived(cfw.at[0], ss_prev.at[1, n])

    @pl.loop(0, 8)
    def _(j):
        arrived(ob.at[j], ss_o.at[j])

    arrived(ob.at[8 + c], ss_o.at[9])


def body(outer, table, bq, bk, bv, gain, doc, wq, wk, wv):
    vmem = pl.BlockSpec(memory_space=pltpu.VMEM)
    anyw = pl.BlockSpec(memory_space=pl.ANY)
    dma = pltpu.SemaphoreType.DMA
    return pl.pallas_call(
        functools.partial(kernel, outer),
        out_shape=(
            jax.ShapeDtypeStruct((ROWS, HEADS * BASED_DIM), BF16),
            jax.ShapeDtypeStruct((ROWS, WIN_HEADS * HEAD_DIM), BF16),
        ),
        in_specs=[vmem] * 6 + [anyw] * 3,
        out_specs=(vmem, anyw),
        scratch_shapes=[
            pltpu.VMEM((2, 16, 2, 128, 128), BF16),
            pltpu.VMEM((2, 2, 128, 128), BF16),
            pltpu.VMEM((10, 128, 128), BF16),
            pltpu.VMEM((10, 128, 128), BF16),
            pltpu.VMEM((8, 8, 128), F32),
            pltpu.VMEM((BACK + 1, 8, 128), F32),
            pltpu.VMEM((16, 128), F32),
            pltpu.VMEM((8 * SLICE, 128), BF16),
            pltpu.VMEM((8, SLICE, 128), BF16),
            pltpu.VMEM((SLICE, 128), F32),
            pltpu.VMEM((BACK, SLICE, 128), F32),
            pltpu.VMEM((8, SLICE, 128), BF16),
            pltpu.VMEM((8 * SLICE, 128), BF16),
            pltpu.VMEM((PAIRS, 128, 128), F32),
            pltpu.VMEM((128, HEADS * 128), BF16),
            dma((2, 8, 2)), dma((2, 8, 2)), dma((2, 8)), dma((2, 8)),
            dma((10,)), dma((10,)), dma((10,)), dma((10,)), dma((2, 2)), dma((2, 2)),
            dma((8,)), dma((8,)), dma((BACK + 1,)), dma((BACK + 1,)),
            dma((8,)), dma((8,)), dma((BACK + 1,)), dma((BACK + 1,)), dma((8,)), dma((8,)),
        ],
        compiler_params=pltpu.CompilerParams(
            collective_id=0, has_side_effects=True, vmem_limit_bytes=40 << 20
        ),
        name="hybrid_attention",
    )(bq, bk, bv, gain.reshape(1, -1), doc.reshape(1, -1), jnp.asarray(table), wq, wk, wv)


def solution(mesh):
    tokens = P(("outer", "inner"), None)
    return jax.shard_map(
        functools.partial(body, mesh.shape["outer"], feature_table()),
        mesh=mesh,
        in_specs=(tokens, tokens, tokens, P(), P(("outer", "inner")), tokens, tokens, tokens),
        out_specs=(tokens, tokens),
        check_vma=False,
    )
```

```python
import functools
import math

import jax
import jax.numpy as jnp
import numpy as np
from jax import lax
from jax.experimental import pallas as pl
from jax.experimental.pallas import tpu as pltpu
from jax.sharding import PartitionSpec as P

HEADS = 10
BASED_DIM = 64
HEAD_DIM = 128
QK_DIM = 11
WIN_HEADS = 10
ROWS = 128
BACK = 8
FEAT = 80
PAIRS = HEADS // 2
SLICE = 64
MESSAGE = SLICE + 16
MESH = pl.DeviceIdType.MESH
ORDER = ((0, 1), (1, 0), (1, 1), (3, 0), (3, 1), (2, 0), (2, 1))
FAR = ORDER[1:]
NT = (((1,), (1,)), ((), ()))
TN = (((0,), (0,)), ((), ()))
F32 = jnp.float32
BF16 = jnp.bfloat16


def feature_table():
    table = np.zeros((8, HEADS * 128), np.float32)
    table[:2] = -1.0
    for head in range(HEADS):
        at = head * 128
        for a in range(QK_DIM + 1):
            for b in range(a, QK_DIM + 1):
                for row, entry in ((0, a), (1, b)):
                    if entry == 0:
                        table[row + 2, at] = 1.0
                    else:
                        table[row, at] = head * QK_DIM + entry - 1
                table[4, at] = 1.0 if a == b else 2.0
                at += 1
    return table


def kernel(
    outer,
    bq_hbm, bk_hbm, bv_hbm, gain_hbm, doc_hbm, aux_hbm, wq_hbm, wk_hbm, wv_hbm,
    bout, wout,
    bq, bk, bv, gain, doc, aux, wq, wk, wv,
    sq, skv, kv, cfw, qb, ob, d2, ssend, srecv, tsend, trecv, fsend, pf, tot, phq,
    ld, rs_own, ss_own, rs_prev, ss_prev, rs_q, ss_q, rs_o, ss_o, rs_c, ss_c,
    rs_s, ss_s, rs_t, ss_t, rs_f, ss_f,
):
    r = lax.axis_index("outer")
    i = lax.axis_index("inner")
    x = i // 2
    c = i % 2
    up = lax.rem(r + 1, outer)
    sib = x * 2 + (1 - c)

    loads = [
        pltpu.make_async_copy(src, dst, ld.at[n])
        for n, (src, dst) in enumerate(
            (
                (doc_hbm, doc), (bk_hbm, bk), (aux_hbm, aux), (bv_hbm, bv),
                (wk_hbm, wk), (wv_hbm, wv), (wq_hbm, wq), (bq_hbm, bq), (gain_hbm, gain),
            )
        )
    ]
    for load in loads:
        load.start()

    def to(dx, dc):
        return lax.rem(x + dx, 4) * 2 + lax.rem(c + dc, 2)

    def frm(dx, dc):
        return lax.rem(x + 4 - dx, 4) * 2 + lax.rem(c + dc, 2)

    def cols(ref, head):
        return ref.at[:, pl.ds(pl.multiple_of(head * HEAD_DIM, HEAD_DIM), HEAD_DIM)]

    def remote(src, dst, ss, rs, row, inner):
        return pltpu.make_async_remote_copy(
            src_ref=src, dst_ref=dst, send_sem=ss, recv_sem=rs,
            device_id=(row, inner), device_id_type=MESH,
        )

    def arrived(dst, rs):
        pltpu.make_async_copy(dst, dst, rs).wait()

    sent = []

    def send(src, dst, ss, rs, row, inner):
        remote(src, dst, ss, rs, row, inner).start()
        sent.append((src, ss))

    barrier = pltpu.get_barrier_semaphore()
    for dx, dc in ORDER:
        pl.semaphore_signal(barrier, inc=1, device_id=(r, to(dx, dc)), device_id_type=MESH)
    for k in range(1, BACK + 1):
        pl.semaphore_signal(
            barrier, inc=1, device_id=(lax.rem(r + outer - k, outer), i), device_id_type=MESH
        )

    for load in loads[:4]:
        load.wait()
    doc_row = doc[...].astype(F32)
    table = aux[...]
    place = lax.broadcasted_iota(jnp.int32, (QK_DIM * HEADS, HEADS * 128), 0).astype(F32)
    pick_a = jnp.where(place == table[0:1, :], 0.5, 0.0).astype(BF16)
    pick_b = jnp.where(place == table[1:2, :], 0.5, 0.0).astype(BF16)
    xk = bk[...]

    def features(proj):
        first = lax.dot_general(proj, pick_a, TN, preferred_element_type=F32) + table[2:3, :]
        second = lax.dot_general(proj, pick_b, TN, preferred_element_type=F32) + table[3:4, :]
        return first * second

    lane = lax.broadcasted_iota(jnp.int32, (128, 128), 1)
    row = lax.broadcasted_iota(jnp.int32, (128, 128), 0)
    left = lane < BASED_DIM
    own_rows = jnp.broadcast_to(doc_row, (128, 128))
    own_cols = own_rows.T
    keep = own_cols == doc_row[:, 127:128]
    fk = features(xk).astype(BF16)
    docs_tail = jnp.broadcast_to(doc_row, (16, 128)).astype(BF16)
    for p in range(PAIRS):
        vals = bv[:, p * 128 : (p + 1) * 128]
        kept = jnp.where(keep, vals.astype(F32), 0.0).astype(BF16)
        both = [
            lax.dot_general(
                fk[:, h * 128 : (h + 1) * 128], kept, TN, preferred_element_type=F32
            )
            for h in (2 * p, 2 * p + 1)
        ]
        state = jnp.where(left, both[0], both[1]).astype(BF16)
        for q in range(FEAT // 16):
            at = p * (FEAT // 16) + q
            ssend[at // 4, (at % 4) * 16 : (at % 4 + 1) * 16, :] = state[q * 16 : (q + 1) * 16]
    for at in range(PAIRS * FEAT // 16, 8 * SLICE // 16):
        ssend[at // 4, (at % 4) * 16 : (at % 4 + 1) * 16, :] = jnp.zeros((16, 128), BF16)
    for s in range(8):
        ssend[s, SLICE:MESSAGE, :] = docs_tail
    srecv[i] = ssend[i]

    for load in loads[4:6]:
        load.wait()
    for h in range(WIN_HEADS):
        skv[h, 0] = wk[:, h * 128 : (h + 1) * 128]
        skv[h, 1] = wv[:, h * 128 : (h + 1) * 128]

    pl.semaphore_wait(barrier, len(ORDER) + BACK)

    for n, (dx, dc) in enumerate(ORDER):
        d = to(dx, dc)
        send(ssend.at[d], srecv.at[i], ss_s.at[n], rs_s.at[i], r, d)
    send(skv.at[8:10], cfw, ss_c, rs_c, up, i)
    for n, (dx, dc) in enumerate(ORDER):
        d = to(dx, dc)
        send(skv.at[d], kv.at[0, 8 + i], ss_own.at[0, n], rs_own.at[0, i], r, d)
    send(skv.at[i], kv.at[0, i], ss_prev.at[0, i], rs_prev.at[0, i], up, i)
    for load in loads[6:]:
        load.wait()
    for h in range(WIN_HEADS):
        sq[h] = wq[:, h * 128 : (h + 1) * 128]
    send(sq.at[9 - c], qb.at[8 + c], ss_q.at[7], rs_q.at[8 + c], r, sib)
    send(skv.at[9 - c], kv.at[1, 8 + i], ss_own.at[1, 0], rs_own.at[1, i], r, sib)
    kv[0, 8 + i] = skv[i]
    kv[1, 8 + i] = skv[8 + c]
    qb[i] = sq[i]
    qb[8 + c] = sq[8 + c]

    sub = lax.broadcasted_iota(jnp.int32, (8, 128), 0)
    for dx, dc in ORDER:
        s = frm(dx, dc)
        arrived(srecv.at[s], rs_s.at[s])
    row_docs = jnp.zeros((8, 128), F32)
    for s in range(8):
        tail = srecv[s, SLICE:MESSAGE, :].astype(F32)
        row_docs = jnp.where(sub == s, tail[0:8], row_docs)
    last = [row_docs[s : s + 1, 127:128] for s in range(8)]
    acc = srecv[0, :SLICE, :].astype(F32)
    running = []
    for s in range(1, 8):
        running.append(acc)
        acc = srecv[s, :SLICE, :].astype(F32) + jnp.where(last[s] == last[s - 1], acc, 0.0)
    tsend[:SLICE, :] = acc.astype(BF16)
    tsend[SLICE:, :] = jnp.concatenate([row_docs, row_docs], axis=0).astype(BF16)
    for k in range(1, BACK + 1):
        send(tsend, trecv.at[k - 1], ss_t.at[k], rs_t.at[k], lax.rem(r + k, outer), i)

    arrived(cfw, rs_c)
    kv[1, i] = cfw[c]
    send(cfw.at[1 - c], kv.at[1, i], ss_prev.at[1, 0], rs_prev.at[1, i], r, sib)
    for n, (dx, dc) in enumerate(FAR):
        h = lax.rem(c + dc, 2)
        d = to(dx, dc)

        @pl.when(x + dx < 4)
        def _():
            remote(
                skv.at[8 + h], kv.at[1, 8 + i], ss_own.at[1, n + 1], rs_own.at[1, i], r, d
            ).start()

        @pl.when(x + dx >= 4)
        def _():
            remote(
                cfw.at[h], kv.at[1, i], ss_prev.at[1, n + 1], rs_prev.at[1, i], r, d
            ).start()

    for n, (dx, dc) in enumerate(ORDER):
        s = frm(dx, dc)
        arrived(kv.at[0, 8 + s], rs_own.at[0, s])
        send(kv.at[0, 8 + s], kv.at[0, s], ss_prev.at[0, s], rs_prev.at[0, s], up, i)
    for n, (dx, dc) in enumerate(ORDER):
        d = to(dx, dc)
        send(sq.at[d], qb.at[i], ss_q.at[n], rs_q.at[i], r, d)

    before = []
    for k in range(1, BACK + 1):
        arrived(trecv.at[k - 1], rs_t.at[k])
        before.append(trecv[k - 1, SLICE:MESSAGE, :].astype(F32)[0:8])
    entering_doc = jnp.where(r >= 1, before[0][7:8, 127:128], -1.0)
    enter = jnp.zeros((SLICE, 128), F32)
    for k in range(1, BACK + 1):
        same = jnp.where(r >= k, before[k - 1][7:8, 127:128], -2.0) == entering_doc
        enter = enter + jnp.where(same, trecv[k - 1, :SLICE, :].astype(F32), 0.0)
    fsend[0] = enter.astype(BF16)
    for s in range(1, 8):
        fsend[s] = (running[s - 1] + jnp.where(last[s - 1] == entering_doc, enter, 0.0)).astype(BF16)

    def block(ref, d):
        return ref.at[pl.ds(pl.multiple_of(d * SLICE, SLICE), SLICE)]

    for n, (dx, dc) in enumerate(ORDER):
        d = to(dx, dc)
        send(fsend.at[d], block(pf, i), ss_f.at[n], rs_f.at[i], r, d)
    pf[pl.ds(pl.multiple_of(i * SLICE, SLICE), SLICE), :] = fsend[i]
    d2[0:8] = jnp.where(r >= 1, before[0], -1.0)
    d2[8:16] = row_docs

    xq = bq[...]
    inside = (own_cols == own_rows) & (lane <= row)
    lane_q = lax.broadcasted_iota(jnp.int32, (QK_DIM * HEADS, 128), 0)
    for p in range(PAIRS):
        vals = bv[:, p * 128 : (p + 1) * 128]
        both = []
        for h in (2 * p, 2 * p + 1):
            mine = (lane_q >= h * QK_DIM) & (lane_q < (h + 1) * QK_DIM)
            part_q = jnp.where(mine, xq.astype(F32), 0.0).astype(BF16)
            dots = lax.dot_general(part_q, xk, TN, preferred_element_type=F32) * 0.25 + 1.0
            weight = jnp.where(inside, dots * dots, 0.0).astype(BF16)
            both.append(jnp.dot(weight, vals, preferred_element_type=F32))
        tot[p] = jnp.where(left, both[0], both[1])
    phq[...] = (features(xq) * table[4:5, :]).astype(BF16)

    factor = math.log2(math.e) / math.sqrt(HEAD_DIM)

    def attend(b, j, at):
        query = qb[at]
        docq = jnp.broadcast_to(d2[pl.ds(8 + j, 1), :], (128, 128)).T
        scores = []
        top = None
        for t in range(BACK + 1):
            block_scores = lax.dot_general(
                query, kv[b, j + t, 0], NT, preferred_element_type=F32
            )
            see = docq == d2[pl.ds(j + t, 1), :]
            if t == 0:
                see = see & (lane > row)
            if t == BACK:
                see = see & (lane <= row)
            block_scores = jnp.where(see, block_scores, -1e30)
            scores.append(block_scores)
            top = block_scores if top is None else jnp.maximum(top, block_scores)
        peak = jnp.max(top, axis=1, keepdims=True)
        whole = None
        mixed = None
        for t in range(BACK + 1):
            prob = jnp.exp2((scores[t] - peak) * factor)
            whole = prob if whole is None else whole + prob
            term = jnp.dot(prob.astype(BF16), kv[b, j + t, 1], preferred_element_type=F32)
            mixed = term if mixed is None else mixed + term
        rowsum = jnp.sum(whole, axis=1, keepdims=True)
        ob[at] = (mixed / rowsum).astype(BF16)

    arrived(qb.at[9 - c], rs_q.at[9 - c])

    @pl.loop(0, 2 * x + 2)
    def _(s):
        @pl.when(s != i)
        def _():
            arrived(kv.at[1, 8 + s], rs_own.at[1, s])

    @pl.loop(2 * x, 8)
    def _(s):
        @pl.when(s != i)
        def _():
            arrived(kv.at[1, s], rs_prev.at[1, s])

    @pl.loop(0, 2)
    def _(core):
        attend(1, 2 * x + core, 8 + core)

    send(ob.at[9 - c], cols(wout, 8 + c), ss_o.at[8], rs_o.at[8 + c], r, sib)
    pltpu.make_async_copy(ob.at[8 + c], cols(wout, 8 + c), ss_o.at[9]).start()

    @pl.loop(0, 8)
    def _(step):
        j = 7 - step

        @pl.when(j != i)
        def _():
            arrived(qb.at[j], rs_q.at[j])

        arrived(kv.at[0, j], rs_prev.at[0, j])
        attend(0, j, j)

        @pl.when(j != i)
        def _():
            remote(ob.at[j], cols(wout, i), ss_o.at[j], rs_o.at[i], r, j).start()

        @pl.when(j == i)
        def _():
            pltpu.make_async_copy(ob.at[j], cols(wout, i), ss_o.at[j]).start()

    for dx, dc in ORDER:
        s = frm(dx, dc)
        arrived(block(pf, s), rs_f.at[s])
    previous = jnp.where(i == 0, entering_doc, -1.0)
    for s in range(1, 8):
        previous = jnp.where(i == s, last[s - 1], previous)
    carried = own_cols == previous
    rest = jnp.zeros((128 - FEAT, 128), BF16)
    for p in range(PAIRS):
        state = jnp.concatenate([pf[p * FEAT : (p + 1) * FEAT, :], rest], axis=0)
        both = [
            jnp.dot(phq[:, h * 128 : (h + 1) * 128], state, preferred_element_type=F32)
            for h in (2 * p, 2 * p + 1)
        ]
        total = tot[p] + jnp.where(carried, jnp.where(left, both[0], both[1]), 0.0)
        square = total * total
        one = jnp.sum(jnp.where(left, square, 0.0), axis=1, keepdims=True)
        two = jnp.sum(jnp.where(left, 0.0, square), axis=1, keepdims=True)
        mean = jnp.where(left, one, two) * (1.0 / BASED_DIM)
        scaled = total * lax.rsqrt(mean + 1e-5) * gain[p * 128 : (p + 1) * 128].reshape(1, 128)
        bout[:, p * 128 : (p + 1) * 128] = scaled.astype(BF16)

    @pl.loop(0, 8)
    def _(j):
        @pl.when(j != i)
        def _():
            arrived(cols(wout, j), rs_o.at[j])

    arrived(cols(wout, 9 - c), rs_o.at[9 - c])
    for src, ss in sent:
        arrived(src, ss)
    for n, (dx, dc) in enumerate(FAR):

        @pl.when(x + dx < 4)
        def _():
            arrived(kv.at[1, 8 + i], ss_own.at[1, n + 1])

        @pl.when(x + dx >= 4)
        def _():
            arrived(cfw.at[0], ss_prev.at[1, n + 1])

    @pl.loop(0, 8)
    def _(j):
        arrived(ob.at[j], ss_o.at[j])

    arrived(ob.at[8 + c], ss_o.at[9])


def body(outer, table, bq, bk, bv, gain, doc, wq, wk, wv):
    vmem = pl.BlockSpec(memory_space=pltpu.VMEM)
    anyw = pl.BlockSpec(memory_space=pl.ANY)
    dma = pltpu.SemaphoreType.DMA
    operands = (bq.T, bk.T, bv, gain, doc.reshape(1, -1), jnp.asarray(table), wq, wk, wv)
    return pl.pallas_call(
        functools.partial(kernel, outer),
        out_shape=(
            jax.ShapeDtypeStruct((ROWS, HEADS * BASED_DIM), BF16),
            jax.ShapeDtypeStruct((ROWS, WIN_HEADS * HEAD_DIM), BF16),
        ),
        in_specs=[anyw] * 9,
        out_specs=(vmem, anyw),
        scratch_shapes=[pltpu.VMEM(a.shape, a.dtype) for a in operands]
        + [
            pltpu.VMEM((10, 128, 128), BF16),
            pltpu.VMEM((10, 2, 128, 128), BF16),
            pltpu.VMEM((2, 16, 2, 128, 128), BF16),
            pltpu.VMEM((2, 2, 128, 128), BF16),
            pltpu.VMEM((10, 128, 128), BF16),
            pltpu.VMEM((10, 128, 128), BF16),
            pltpu.VMEM((16, 128), F32),
            pltpu.VMEM((8, MESSAGE, 128), BF16),
            pltpu.VMEM((8, MESSAGE, 128), BF16),
            pltpu.VMEM((MESSAGE, 128), BF16),
            pltpu.VMEM((BACK, MESSAGE, 128), BF16),
            pltpu.VMEM((8, SLICE, 128), BF16),
            pltpu.VMEM((8 * SLICE, 128), BF16),
            pltpu.VMEM((PAIRS, 128, 128), F32),
            pltpu.VMEM((128, HEADS * 128), BF16),
            dma((9,)), dma((2, 8)), dma((2, 8)), dma((2, 8)), dma((2, 8)),
            dma((10,)), dma((10,)), dma((10,)), dma((10,)), dma, dma,
            dma((8,)), dma((8,)), dma((BACK + 1,)), dma((BACK + 1,)), dma((8,)), dma((8,)),
        ],
        compiler_params=pltpu.CompilerParams(
            collective_id=0, has_side_effects=True, vmem_limit_bytes=60 << 20
        ),
        name="hybrid_attention",
    )(*operands)


def solution(mesh):
    tokens = P(("outer", "inner"), None)
    return jax.shard_map(
        functools.partial(body, mesh.shape["outer"], feature_table()),
        mesh=mesh,
        in_specs=(tokens, tokens, tokens, P(), P(("outer", "inner")), tokens, tokens, tokens),
        out_specs=(tokens, tokens),
        check_vma=False,
    )
```

```python
import functools
import math

import jax
import jax.numpy as jnp
import numpy as np
from jax import lax
from jax.experimental import pallas as pl
from jax.experimental.pallas import tpu as pltpu
from jax.sharding import PartitionSpec as P

HEADS = 10
BASED_DIM = 64
HEAD_DIM = 128
QK_DIM = 11
WIN_HEADS = 10
ROWS = 128
BACK = 8
PLANE = 4
PAIRS = HEADS // 2
GROUP = 13
GROUPS = 6
FEAT = GROUPS * 16
PLANE_DEVS = 32
MESH = pl.DeviceIdType.MESH
ORDER = ((0, 1), (1, 0), (1, 1), (3, 0), (3, 1), (2, 0), (2, 1))
FAR = ORDER[1:]
NT = (((1,), (1,)), ((), ()))
TN = (((0,), (0,)), ((), ()))
F32 = jnp.float32
BF16 = jnp.bfloat16


def feature_table():
    table = np.zeros((8, HEADS * 128), np.float32)
    table[:2] = -1.0
    for head in range(HEADS):
        feature = 0
        for a in range(QK_DIM + 1):
            for b in range(a, QK_DIM + 1):
                at = head * 128 + feature // GROUP * 16 + feature % GROUP
                for row, entry in ((0, a), (1, b)):
                    if entry == 0:
                        table[row + 2, at] = 1.0
                    else:
                        table[row, at] = head * QK_DIM + entry - 1
                table[4, at] = 1.0 if a == b else 2.0
                feature += 1
    return table


def kernel(
    outer,
    bq_hbm, bk_hbm, bv_hbm, gain_hbm, doc_hbm, aux_hbm, wq_hbm, wk_hbm, wv_hbm,
    bout, wout,
    bq, bk, bv, gain, doc, aux, wq, wk, wv,
    sq, skv, kv, cfw, qb, ob, d2, ssend, srecv, running, plane_docs, wsend, wrecv, fsend, pf, tot, phq,
    peaks, sums, mixes,
    ld, rs_own, ss_own, rs_prev, ss_prev, rs_q, ss_q, rs_o, ss_o, rs_c, ss_c,
    rs_s, ss_s, rs_w, ss_w, rs_f, ss_f,
):
    r = lax.axis_index("outer")
    i = lax.axis_index("inner")
    x = i // 2
    c = i % 2
    z = r // PLANE
    y = r % PLANE
    me = y * 8 + i
    up = lax.rem(r + 1, outer)
    sib = x * 2 + (1 - c)

    loads = [
        pltpu.make_async_copy(src, dst, ld.at[n])
        for n, (src, dst) in enumerate(
            (
                (doc_hbm, doc), (bk_hbm, bk), (aux_hbm, aux), (bv_hbm, bv),
                (wk_hbm, wk), (wv_hbm, wv), (wq_hbm, wq), (bq_hbm, bq), (gain_hbm, gain),
            )
        )
    ]
    for load in loads:
        load.start()

    def to(dx, dc):
        return lax.rem(x + dx, 4) * 2 + lax.rem(c + dc, 2)

    plane_rows = [lax.rem(y + k, PLANE) for k in range(PLANE)]
    plane_outer = [z * PLANE + k for k in plane_rows]
    plane_inner = [lax.rem(i + k, 8) for k in range(8)]
    others = [
        (plane_rows[n // 8] * 8 + plane_inner[n % 8], plane_outer[n // 8], plane_inner[n % 8])
        for n in range(1, PLANE_DEVS)
    ]

    def frm(dx, dc):
        return lax.rem(x + 4 - dx, 4) * 2 + lax.rem(c + dc, 2)

    def cols(ref, head):
        return ref.at[:, pl.ds(pl.multiple_of(head * HEAD_DIM, HEAD_DIM), HEAD_DIM)]

    def remote(src, dst, ss, rs, row, inner):
        return pltpu.make_async_remote_copy(
            src_ref=src, dst_ref=dst, send_sem=ss, recv_sem=rs,
            device_id=(row, inner), device_id_type=MESH,
        )

    def arrived(dst, rs):
        pltpu.make_async_copy(dst, dst, rs).wait()

    sent = []

    def send(src, dst, ss, rs, row, inner):
        remote(src, dst, ss, rs, row, inner).start()
        sent.append((src, ss))

    barrier = pltpu.get_barrier_semaphore()
    for dx, dc in ORDER:
        pl.semaphore_signal(barrier, inc=1, device_id=(r, to(dx, dc)), device_id_type=MESH)
    senders = [lax.rem(r + outer - 1, outer)]
    senders += [lax.rem(r + outer - k * PLANE, outer) for k in (1, 2)]
    for other in senders:
        pl.semaphore_signal(barrier, inc=1, device_id=(other, i), device_id_type=MESH)

    for _, row, inner in others[7:]:
        pl.semaphore_signal(barrier, inc=1, device_id=(row, inner), device_id_type=MESH)


    for load in loads[:4]:
        load.wait()
    doc_row = doc[...].astype(F32)
    table = aux[...]
    place = lax.broadcasted_iota(jnp.int32, (QK_DIM * HEADS, HEADS * 128), 0).astype(F32)
    pick_a = jnp.where(place == table[0:1, :], 0.5, 0.0).astype(BF16)
    pick_b = jnp.where(place == table[1:2, :], 0.5, 0.0).astype(BF16)
    xk = bk[...]

    def features(proj):
        first = lax.dot_general(proj, pick_a, TN, preferred_element_type=F32) + table[2:3, :]
        second = lax.dot_general(proj, pick_b, TN, preferred_element_type=F32) + table[3:4, :]
        return first * second

    lane = lax.broadcasted_iota(jnp.int32, (128, 128), 1)
    row = lax.broadcasted_iota(jnp.int32, (128, 128), 0)
    left = lane < BASED_DIM
    own_rows = jnp.broadcast_to(doc_row, (128, 128))
    own_cols = own_rows.T
    keep = own_cols == doc_row[:, 127:128]
    fk = features(xk).astype(BF16)
    docs_tail = jnp.broadcast_to(doc_row, (16, 128))
    tail = lax.broadcasted_iota(jnp.int32, (16, 128), 0) >= GROUP
    for p in range(PAIRS):
        vals = bv[:, p * 128 : (p + 1) * 128]
        kept = jnp.where(keep, vals.astype(F32), 0.0).astype(BF16)
        both = [
            lax.dot_general(
                fk[:, h * 128 : (h + 1) * 128], kept, TN, preferred_element_type=F32
            )
            for h in (2 * p, 2 * p + 1)
        ]
        state = jnp.where(left, both[0], both[1])
        for q in range(GROUPS):
            ssend[p * GROUPS + q] = jnp.where(
                tail, docs_tail, state[q * 16 : (q + 1) * 16]
            ).astype(BF16)
    for q in range(PAIRS * GROUPS, PLANE_DEVS):
        ssend[q] = docs_tail.astype(BF16)
    srecv[me] = ssend[me]

    for load in loads[4:6]:
        load.wait()
    for h in range(WIN_HEADS):
        skv[h, 0] = wk[:, h * 128 : (h + 1) * 128]
        skv[h, 1] = wv[:, h * 128 : (h + 1) * 128]

    pl.semaphore_wait(barrier, PLANE_DEVS - 1 + len(senders))

    for n, (place, outer_at, inner_at) in enumerate(others):
        remote(ssend.at[place], srecv.at[me], ss_s.at[n], rs_s.at[me], outer_at, inner_at).start()
    send(skv.at[8:10], cfw, ss_c, rs_c, up, i)
    send(skv.at[i], kv.at[0, i], ss_prev.at[0, i], rs_prev.at[0, i], up, i)

    def send_kv(steps):
        for n in steps:
            d = to(*ORDER[n])
            send(skv.at[d], kv.at[0, 8 + i], ss_own.at[0, n], rs_own.at[0, i], r, d)

    def pass_on(steps):
        for n in steps:
            s = frm(*ORDER[n])
            arrived(kv.at[0, 8 + s], rs_own.at[0, s])
            send(kv.at[0, 8 + s], kv.at[0, s], ss_prev.at[0, s], rs_prev.at[0, s], up, i)

    send_kv(range(5))
    for load in loads[6:]:
        load.wait()
    for h in range(WIN_HEADS):
        sq[h] = wq[:, h * 128 : (h + 1) * 128]
    send(sq.at[9 - c], qb.at[8 + c], ss_q.at[7], rs_q.at[8 + c], r, sib)
    send(skv.at[9 - c], kv.at[1, 8 + i], ss_own.at[1, 0], rs_own.at[1, i], r, sib)
    kv[0, 8 + i] = skv[i]
    kv[1, 8 + i] = skv[8 + c]
    qb[i] = sq[i]
    qb[8 + c] = sq[8 + c]

    pass_on(range(1))

    for place, _, _ in others:
        arrived(srecv.at[place], rs_s.at[place])

    messages = [srecv[k].astype(F32) for k in range(PLANE_DEVS)]
    last = [message[GROUP : GROUP + 1, 127:128] for message in messages]
    acc = messages[0]
    for k in range(1, PLANE_DEVS):
        running[k] = acc
        acc = messages[k] + jnp.where(last[k] == last[k - 1], acc, 0.0)
    sub = lax.broadcasted_iota(jnp.int32, (8, 128), 0)
    for k in range(PLANE):
        docs = jnp.zeros((8, 128), F32)
        for m in range(8):
            docs = jnp.where(sub == m, messages[k * 8 + m][GROUP : GROUP + 1, :], docs)
        plane_docs[k] = docs
    wsend[:16, :] = acc.astype(BF16)
    wsend[16:, :] = jnp.concatenate([docs, docs], axis=0).astype(BF16)
    for k in (1, 2):
        send(wsend, wrecv.at[k - 1], ss_w.at[k], rs_w.at[k], lax.rem(r + k * PLANE, outer), i)

    send_kv(range(5, 7))
    arrived(cfw, rs_c)
    kv[1, i] = cfw[c]
    send(cfw.at[1 - c], kv.at[1, i], ss_prev.at[1, 0], rs_prev.at[1, i], r, sib)
    pass_on(range(1, 5))
    for n, (dx, dc) in enumerate(ORDER):
        d = to(dx, dc)
        send(sq.at[d], qb.at[i], ss_q.at[n], rs_q.at[i], r, d)

    for n, (dx, dc) in enumerate(FAR):
        h = lax.rem(c + dc, 2)
        d = to(dx, dc)

        @pl.when(x + dx < 4)
        def _():
            remote(
                skv.at[8 + h], kv.at[1, 8 + i], ss_own.at[1, n + 1], rs_own.at[1, i], r, d
            ).start()

        @pl.when(x + dx >= 4)
        def _():
            remote(
                cfw.at[h], kv.at[1, i], ss_prev.at[1, n + 1], rs_prev.at[1, i], r, d
            ).start()

    pass_on(range(5, 7))

    xq = bq[...]
    inside = (own_cols == own_rows) & (lane <= row)
    lane_q = lax.broadcasted_iota(jnp.int32, (QK_DIM * HEADS, 128), 0)
    for p in range(PAIRS):
        vals = bv[:, p * 128 : (p + 1) * 128]
        both = []
        for h in (2 * p, 2 * p + 1):
            mine = (lane_q >= h * QK_DIM) & (lane_q < (h + 1) * QK_DIM)
            part_q = jnp.where(mine, xq.astype(F32), 0.0).astype(BF16)
            dots = lax.dot_general(part_q, xk, TN, preferred_element_type=F32) * 0.25 + 1.0
            weight = jnp.where(inside, dots * dots, 0.0).astype(BF16)
            both.append(jnp.dot(weight, vals, preferred_element_type=F32))
        tot[p] = jnp.where(left, both[0], both[1])
    phq[...] = (features(xq) * table[4:5, :]).astype(BF16)

    factor = math.log2(math.e) / math.sqrt(HEAD_DIM)
    own_docs = plane_docs[y]
    for k in range(8):
        d2[:, (8 + k) * 128 : (9 + k) * 128] = own_docs[k : k + 1]

    def doc_span(slot, count):
        return d2[:, pl.ds(pl.multiple_of(slot * 128, 128), count * 128)]

    def weigh(query, b, slot, count, low, high, start):
        docq = jnp.broadcast_to(query[1], (128, 128)).T[:, 0:1]
        keys = kv[b, pl.ds(slot, count), 0].reshape(count * 128, 128)
        scores = lax.dot_general(query[0], keys, NT, preferred_element_type=F32)
        off = lax.broadcasted_iota(jnp.int32, scores.shape, 1) - lax.broadcasted_iota(
            jnp.int32, scores.shape, 0
        )
        see = docq == doc_span(slot, count)
        if low is not None:
            see = see & (off > low)
        if high is not None:
            see = see & (off <= high)
        scores = jnp.where(see, scores, -1e30)
        peak = jnp.max(scores, axis=1, keepdims=True)
        if start is not None:
            peak = jnp.maximum(peak, start)
        prob = jnp.exp2((scores - peak) * factor)
        rowsum = jnp.sum(prob, axis=1, keepdims=True)
        values = kv[b, pl.ds(slot, count), 1].reshape(count * 128, 128)
        mixed = jnp.dot(prob.astype(BF16), values, preferred_element_type=F32)
        return peak, rowsum, mixed

    def attend(b, j, at):
        _, rowsum, mixed = weigh(
            (qb[at], doc_span(8 + j, 1)), b, j, BACK + 1, 0, BACK * 128, None
        )
        ob[at] = (mixed / rowsum).astype(BF16)

    def own_part(j, count):
        peak, rowsum, mixed = weigh(
            (qb[j], doc_span(8 + j, 1)), 0, 8, count, None, j * 128, None
        )
        peaks[j] = jnp.broadcast_to(peak, (128, 128))
        sums[j] = jnp.broadcast_to(rowsum, (128, 128))
        mixes[j] = mixed

    def last_part(j, first):
        before = peaks[j]
        peak, rowsum, mixed = weigh(
            (qb[j], doc_span(8 + j, 1)), 0, first, 8 - first, (j - first) * 128, None,
            before[:, 0:1],
        )
        fade = jnp.exp2((before - peak) * factor)
        ob[j] = ((mixed + mixes[j] * fade) / (rowsum + sums[j] * fade)).astype(BF16)

    for dx, dc in ORDER:
        s = frm(dx, dc)
        arrived(qb.at[s], rs_q.at[s])

    @pl.loop(4, 8)
    def _(j):
        own_part(j, 8)

    @pl.loop(0, 4)
    def _(j):
        own_part(j, 4)

    for k in (1, 2):
        arrived(wrecv.at[k - 1], rs_w.at[k])
    before = [wrecv[k].astype(F32) for k in range(2)]
    entering_doc = jnp.where(z >= 1, before[0][23:24, 127:128], -1.0)
    enter = jnp.where(z >= 1, before[0][:16], 0.0)
    same = jnp.where(z >= 2, before[1][23:24, 127:128], -2.0) == entering_doc
    enter = enter + jnp.where(same, before[1][:16], 0.0)
    fsend[0] = enter.astype(BF16)
    previous = entering_doc
    for k in range(1, PLANE_DEVS):
        fsend[k] = (running[k] + jnp.where(last[k - 1] == entering_doc, enter, 0.0)).astype(BF16)
        previous = jnp.where(me == k, last[k - 1], previous)

    for n, (place, outer_at, inner_at) in enumerate(others):
        remote(fsend.at[place], pf.at[me], ss_f.at[n], rs_f.at[me], outer_at, inner_at).start()
    pf[me] = fsend[me]
    docs_before = jnp.where(z >= 1, before[0][16:24], -1.0)
    docs_before = jnp.where(y >= 1, plane_docs[jnp.maximum(y - 1, 0)], docs_before)
    for k in range(8):
        d2[:, k * 128 : (k + 1) * 128] = docs_before[k : k + 1]

    def finish(j):
        @pl.when(j != i)
        def _():
            remote(ob.at[j], cols(wout, i), ss_o.at[j], rs_o.at[i], r, j).start()

        @pl.when(j == i)
        def _():
            pltpu.make_async_copy(ob.at[j], cols(wout, i), ss_o.at[j]).start()

    @pl.loop(0, 4)
    def _(step):
        arrived(kv.at[0, 7 - step], rs_prev.at[0, 7 - step])

    @pl.loop(0, 4)
    def _(step):
        last_part(7 - step, 4)
        finish(7 - step)

    @pl.loop(0, 4)
    def _(step):
        arrived(kv.at[0, 3 - step], rs_prev.at[0, 3 - step])

    @pl.loop(0, 4)
    def _(step):
        last_part(3 - step, 0)
        finish(3 - step)

    arrived(qb.at[9 - c], rs_q.at[9 - c])

    @pl.loop(0, 2 * x + 2)
    def _(s):
        @pl.when(s != i)
        def _():
            arrived(kv.at[1, 8 + s], rs_own.at[1, s])

    @pl.loop(2 * x, 8)
    def _(s):
        @pl.when(s != i)
        def _():
            arrived(kv.at[1, s], rs_prev.at[1, s])

    @pl.loop(0, 2)
    def _(step):
        core = lax.rem(1 - c + step, 2)
        attend(1, 2 * x + core, 8 + core)

        @pl.when(step == 0)
        def _():
            remote(ob.at[9 - c], cols(wout, 8 + c), ss_o.at[8], rs_o.at[8 + c], r, sib).start()

    pltpu.make_async_copy(ob.at[8 + c], cols(wout, 8 + c), ss_o.at[9]).start()

    for place, _, _ in others:
        arrived(pf.at[place], rs_f.at[place])

    carried = own_cols == previous
    for p in range(PAIRS):
        state = pf[p * GROUPS : (p + 1) * GROUPS].reshape(FEAT, 128)
        both = [
            jnp.dot(phq[:, h * 128 : h * 128 + FEAT], state, preferred_element_type=F32)
            for h in (2 * p, 2 * p + 1)
        ]
        total = tot[p] + jnp.where(carried, jnp.where(left, both[0], both[1]), 0.0)
        square = total * total
        one = jnp.sum(jnp.where(left, square, 0.0), axis=1, keepdims=True)
        two = jnp.sum(jnp.where(left, 0.0, square), axis=1, keepdims=True)
        mean = jnp.where(left, one, two) * (1.0 / BASED_DIM)
        scaled = total * lax.rsqrt(mean + 1e-5) * gain[p * 128 : (p + 1) * 128].reshape(1, 128)
        bout[:, p * 128 : (p + 1) * 128] = scaled.astype(BF16)

    @pl.loop(0, 8)
    def _(j):
        @pl.when(j != i)
        def _():
            arrived(cols(wout, j), rs_o.at[j])

    arrived(cols(wout, 9 - c), rs_o.at[9 - c])
    for src, ss in sent:
        arrived(src, ss)

    @pl.loop(0, PLANE_DEVS - 1)
    def _(n):
        arrived(ssend.at[0], ss_s.at[n])
        arrived(fsend.at[0], ss_f.at[n])

    for n, (dx, dc) in enumerate(FAR):

        @pl.when(x + dx < 4)
        def _():
            arrived(kv.at[1, 8 + i], ss_own.at[1, n + 1])

        @pl.when(x + dx >= 4)
        def _():
            arrived(cfw.at[0], ss_prev.at[1, n + 1])

    @pl.loop(0, 8)
    def _(j):
        arrived(ob.at[j], ss_o.at[j])

    arrived(ob.at[9 - c], ss_o.at[8])
    arrived(ob.at[8 + c], ss_o.at[9])


def hand_over(based, window, bout, wout, held_based, held_window, sems):
    loads = [
        pltpu.make_async_copy(window, held_window, sems.at[0]),
        pltpu.make_async_copy(based, held_based, sems.at[1]),
    ]
    stores = [
        pltpu.make_async_copy(held_window, wout, sems.at[2]),
        pltpu.make_async_copy(held_based, bout, sems.at[3]),
    ]
    for load in loads:
        load.start()
    for load, store in zip(loads, stores):
        load.wait()
        store.start()
    for store in stores:
        store.wait()


def body(outer, table, bq, bk, bv, gain, doc, wq, wk, wv):
    vmem = pl.BlockSpec(memory_space=pltpu.VMEM)
    anyw = pl.BlockSpec(memory_space=pl.ANY)
    dma = pltpu.SemaphoreType.DMA
    operands = (bq.T, bk.T, bv, gain, doc.reshape(1, -1), jnp.asarray(table), wq, wk, wv)
    parts = pl.pallas_call(
        functools.partial(kernel, outer),
        out_shape=(
            jax.ShapeDtypeStruct((ROWS, HEADS * BASED_DIM), BF16),
            jax.ShapeDtypeStruct((ROWS, WIN_HEADS * HEAD_DIM), BF16),
        ),
        in_specs=[anyw] * 9,
        out_specs=(vmem, anyw),
        scratch_shapes=[pltpu.VMEM(a.shape, a.dtype) for a in operands]
        + [
            pltpu.VMEM((10, 128, 128), BF16),
            pltpu.VMEM((10, 2, 128, 128), BF16),
            pltpu.VMEM((2, 16, 2, 128, 128), BF16),
            pltpu.VMEM((2, 2, 128, 128), BF16),
            pltpu.VMEM((10, 128, 128), BF16),
            pltpu.VMEM((10, 128, 128), BF16),
            pltpu.VMEM((1, 16 * 128), F32),
            pltpu.VMEM((PLANE_DEVS, 16, 128), BF16),
            pltpu.VMEM((PLANE_DEVS, 16, 128), BF16),
            pltpu.VMEM((PLANE_DEVS, 16, 128), F32),
            pltpu.VMEM((PLANE, 8, 128), F32),
            pltpu.VMEM((32, 128), BF16),
            pltpu.VMEM((2, 32, 128), BF16),
            pltpu.VMEM((PLANE_DEVS, 16, 128), BF16),
            pltpu.VMEM((PLANE_DEVS, 16, 128), BF16),
            pltpu.VMEM((PAIRS, 128, 128), F32),
            pltpu.VMEM((128, HEADS * 128), BF16),
            pltpu.VMEM((8, 128, 128), F32),
            pltpu.VMEM((8, 128, 128), F32),
            pltpu.VMEM((8, 128, 128), F32),
            dma((9,)), dma((2, 8)), dma((2, 8)), dma((2, 8)), dma((2, 8)),
            dma((10,)), dma((10,)), dma((10,)), dma((10,)), dma, dma,
            dma((PLANE_DEVS,)), dma((PLANE_DEVS,)), dma((3,)), dma((3,)),
            dma((PLANE_DEVS,)), dma((PLANE_DEVS,)),
        ],
        compiler_params=pltpu.CompilerParams(
            collective_id=0, has_side_effects=True, vmem_limit_bytes=60 << 20
        ),
        name="hybrid_attention",
    )(*operands)
    return pl.pallas_call(
        hand_over,
        out_shape=tuple(jax.ShapeDtypeStruct(a.shape, a.dtype) for a in parts),
        in_specs=[anyw] * 2,
        out_specs=(anyw, anyw),
        scratch_shapes=[pltpu.VMEM(a.shape, a.dtype) for a in parts] + [dma((4,))],
        compiler_params=pltpu.CompilerParams(vmem_limit_bytes=60 << 20),
        name="results",
    )(*parts)


def solution(mesh):
    tokens = P(("outer", "inner"), None)
    return jax.shard_map(
        functools.partial(body, mesh.shape["outer"], feature_table()),
        mesh=mesh,
        in_specs=(tokens, tokens, tokens, P(), P(("outer", "inner")), tokens, tokens, tokens),
        out_specs=(tokens, tokens),
        check_vma=False,
    )
```

```python
import functools
import math

import jax
import jax.numpy as jnp
import numpy as np
from jax import lax
from jax.experimental import pallas as pl
from jax.experimental.pallas import tpu as pltpu
from jax.sharding import PartitionSpec as P

HEADS = 10
BASED_DIM = 64
HEAD_DIM = 128
QK_DIM = 11
WIN_HEADS = 10
ROWS = 128
BACK = 8
PLANE = 4
PAIRS = HEADS // 2
GROUP = 13
GROUPS = 6
FEAT = GROUPS * 16
PLANE_DEVS = 32
MESH = pl.DeviceIdType.MESH
ORDER = ((0, 1), (1, 0), (1, 1), (3, 0), (3, 1), (2, 0), (2, 1))
FAR = ORDER[1:]
NT = (((1,), (1,)), ((), ()))
TN = (((0,), (0,)), ((), ()))
F32 = jnp.float32
BF16 = jnp.bfloat16


def feature_table():
    table = np.zeros((8, HEADS * 128), np.float32)
    table[:2] = -1.0
    for head in range(HEADS):
        feature = 0
        for a in range(QK_DIM + 1):
            for b in range(a, QK_DIM + 1):
                at = head * 128 + feature // GROUP * 16 + feature % GROUP
                for row, entry in ((0, a), (1, b)):
                    if entry == 0:
                        table[row + 2, at] = 1.0
                    else:
                        table[row, at] = head * QK_DIM + entry - 1
                table[4, at] = 1.0 if a == b else 2.0
                feature += 1
    return table


def kernel(
    outer,
    bq_hbm, bk_hbm, bv_hbm, gain_hbm, doc_hbm, aux_hbm, wq_hbm, wk_hbm, wv_hbm,
    bout, wout,
    bq, bk, bv, gain, doc, aux, wq, wk, wv,
    sq, skv, kv, cfw, qb, ob, d2, ssend, srecv, running, plane_docs, wsend, wrecv, fsend, pf, tot, phq,
    peaks, sums, mixes,
    ld, rs_own, ss_own, rs_prev, ss_prev, rs_q, ss_q, rs_o, ss_o, rs_c, ss_c,
    rs_s, ss_s, rs_w, ss_w, rs_f, ss_f,
):
    r = lax.axis_index("outer")
    i = lax.axis_index("inner")
    x = i // 2
    c = i % 2
    z = r // PLANE
    y = r % PLANE
    me = y * 8 + i
    up = lax.rem(r + 1, outer)
    sib = x * 2 + (1 - c)

    def to(dx, dc):
        return lax.rem(x + dx, 4) * 2 + lax.rem(c + dc, 2)

    plane_rows = [lax.rem(y + k, PLANE) for k in range(PLANE)]
    plane_outer = [z * PLANE + k for k in plane_rows]
    plane_inner = [lax.rem(i + k, 8) for k in range(8)]
    others = [
        (plane_rows[n // 8] * 8 + plane_inner[n % 8], plane_outer[n // 8], plane_inner[n % 8])
        for n in range(1, PLANE_DEVS)
    ]

    def frm(dx, dc):
        return lax.rem(x + 4 - dx, 4) * 2 + lax.rem(c + dc, 2)

    def cols(ref, head):
        return ref.at[:, pl.ds(pl.multiple_of(head * HEAD_DIM, HEAD_DIM), HEAD_DIM)]

    def remote(src, dst, ss, rs, row, inner):
        return pltpu.make_async_remote_copy(
            src_ref=src, dst_ref=dst, send_sem=ss, recv_sem=rs,
            device_id=(row, inner), device_id_type=MESH,
        )

    def arrived(dst, rs):
        pltpu.make_async_copy(dst, dst, rs).wait()

    sent = []

    def send(src, dst, ss, rs, row, inner):
        remote(src, dst, ss, rs, row, inner).start()
        sent.append((src, ss))


    barrier = pltpu.get_barrier_semaphore()
    senders = [lax.rem(r + outer - 1, outer)]
    senders += [lax.rem(r + outer - k * PLANE, outer) for k in (2, 1)]
    for other in senders:
        pl.semaphore_signal(barrier, inc=1, device_id=(other, i), device_id_type=MESH)
    for _, row, inner in others[7:]:
        pl.semaphore_signal(barrier, inc=1, device_id=(row, inner), device_id_type=MESH)
    for dx, dc in ORDER:
        pl.semaphore_signal(barrier, inc=1, device_id=(r, to(dx, dc)), device_id_type=MESH)

    loads = [
        pltpu.make_async_copy(src, dst, ld.at[n])
        for n, (src, dst) in enumerate(
            (
                (doc_hbm, doc), (bk_hbm, bk), (aux_hbm, aux), (bv_hbm, bv),
                (wk_hbm, wk), (wv_hbm, wv), (wq_hbm, wq), (bq_hbm, bq), (gain_hbm, gain),
            )
        )
    ]
    for load in loads:
        load.start()


    for load in loads[:4]:
        load.wait()
    doc_row = doc[...].astype(F32)
    table = aux[...]
    place = lax.broadcasted_iota(jnp.int32, (QK_DIM * HEADS, HEADS * 128), 0).astype(F32)
    pick_a = jnp.where(place == table[0:1, :], 0.5, 0.0).astype(BF16)
    pick_b = jnp.where(place == table[1:2, :], 0.5, 0.0).astype(BF16)
    xk = bk[...]

    def features(proj):
        first = lax.dot_general(proj, pick_a, TN, preferred_element_type=F32) + table[2:3, :]
        second = lax.dot_general(proj, pick_b, TN, preferred_element_type=F32) + table[3:4, :]
        return first * second

    lane = lax.broadcasted_iota(jnp.int32, (128, 128), 1)
    row = lax.broadcasted_iota(jnp.int32, (128, 128), 0)
    left = lane < BASED_DIM
    own_rows = jnp.broadcast_to(doc_row, (128, 128))
    own_cols = own_rows.T
    keep = own_cols == doc_row[:, 127:128]
    fk = features(xk).astype(BF16)
    docs_tail = jnp.broadcast_to(doc_row, (16, 128))
    tail = lax.broadcasted_iota(jnp.int32, (16, 128), 0) >= GROUP
    for p in range(PAIRS):
        vals = bv[:, p * 128 : (p + 1) * 128]
        kept = jnp.where(keep, vals.astype(F32), 0.0).astype(BF16)
        both = [
            lax.dot_general(
                fk[:, h * 128 : (h + 1) * 128], kept, TN, preferred_element_type=F32
            )
            for h in (2 * p, 2 * p + 1)
        ]
        state = jnp.where(left, both[0], both[1])
        for q in range(GROUPS):
            ssend[p * GROUPS + q] = jnp.where(
                tail, docs_tail, state[q * 16 : (q + 1) * 16]
            ).astype(BF16)
    for q in range(PAIRS * GROUPS, PLANE_DEVS):
        ssend[q] = docs_tail.astype(BF16)
    srecv[me] = ssend[me]

    for load in loads[4:6]:
        load.wait()
    for h in range(WIN_HEADS):
        skv[h, 0] = wk[:, h * 128 : (h + 1) * 128]
        skv[h, 1] = wv[:, h * 128 : (h + 1) * 128]

    pl.semaphore_wait(barrier, PLANE_DEVS - 1 + len(senders))

    for n, (place, outer_at, inner_at) in enumerate(others):
        remote(ssend.at[place], srecv.at[me], ss_s.at[n], rs_s.at[me], outer_at, inner_at).start()
    send(skv.at[8:10], cfw, ss_c, rs_c, up, i)
    send(skv.at[i], kv.at[0, i], ss_prev.at[0, i], rs_prev.at[0, i], up, i)

    def send_kv(steps):
        for n in steps:
            d = to(*ORDER[n])
            send(skv.at[d], kv.at[0, 8 + i], ss_own.at[0, n], rs_own.at[0, i], r, d)

    def pass_on(steps):
        for n in steps:
            s = frm(*ORDER[n])
            arrived(kv.at[0, 8 + s], rs_own.at[0, s])
            send(kv.at[0, 8 + s], kv.at[0, s], ss_prev.at[0, s], rs_prev.at[0, s], up, i)

    send_kv(range(5))
    for load in loads[6:]:
        load.wait()
    for h in range(WIN_HEADS):
        sq[h] = wq[:, h * 128 : (h + 1) * 128]
    send(sq.at[9 - c], qb.at[8 + c], ss_q.at[7], rs_q.at[8 + c], r, sib)
    send(skv.at[9 - c], kv.at[1, 8 + i], ss_own.at[1, 0], rs_own.at[1, i], r, sib)
    kv[0, 8 + i] = skv[i]
    kv[1, 8 + i] = skv[8 + c]
    qb[i] = sq[i]
    qb[8 + c] = sq[8 + c]

    pass_on(range(1))

    send_kv(range(5, 7))
    arrived(cfw, rs_c)
    kv[1, i] = cfw[c]
    send(cfw.at[1 - c], kv.at[1, i], ss_prev.at[1, 0], rs_prev.at[1, i], r, sib)
    pass_on(range(1, 5))
    for n, (dx, dc) in enumerate(ORDER):
        d = to(dx, dc)
        send(sq.at[d], qb.at[i], ss_q.at[n], rs_q.at[i], r, d)

    pass_on(range(5, 7))
    for place, _, _ in others:
        arrived(srecv.at[place], rs_s.at[place])

    messages = [srecv[k].astype(F32) for k in range(PLANE_DEVS)]
    last = [message[GROUP : GROUP + 1, 127:128] for message in messages]
    acc = messages[0]
    for k in range(1, PLANE_DEVS):
        running[k] = acc
        acc = messages[k] + jnp.where(last[k] == last[k - 1], acc, 0.0)
    sub = lax.broadcasted_iota(jnp.int32, (8, 128), 0)
    for k in range(PLANE):
        docs = jnp.zeros((8, 128), F32)
        for m in range(8):
            docs = jnp.where(sub == m, messages[k * 8 + m][GROUP : GROUP + 1, :], docs)
        plane_docs[k] = docs
    wsend[:16, :] = acc.astype(BF16)
    wsend[16:, :] = jnp.concatenate([docs, docs], axis=0).astype(BF16)
    for k in (1, 2):
        send(wsend, wrecv.at[k - 1], ss_w.at[k], rs_w.at[k], lax.rem(r + k * PLANE, outer), i)

    for n, (dx, dc) in enumerate(FAR):
        h = lax.rem(c + dc, 2)
        d = to(dx, dc)

        @pl.when(x + dx < 4)
        def _():
            remote(
                skv.at[8 + h], kv.at[1, 8 + i], ss_own.at[1, n + 1], rs_own.at[1, i], r, d
            ).start()

        @pl.when(x + dx >= 4)
        def _():
            remote(
                cfw.at[h], kv.at[1, i], ss_prev.at[1, n + 1], rs_prev.at[1, i], r, d
            ).start()


    xq = bq[...]
    inside = (own_cols == own_rows) & (lane <= row)
    lane_q = lax.broadcasted_iota(jnp.int32, (QK_DIM * HEADS, 128), 0)
    for p in range(PAIRS):
        vals = bv[:, p * 128 : (p + 1) * 128]
        both = []
        for h in (2 * p, 2 * p + 1):
            mine = (lane_q >= h * QK_DIM) & (lane_q < (h + 1) * QK_DIM)
            part_q = jnp.where(mine, xq.astype(F32), 0.0).astype(BF16)
            dots = lax.dot_general(part_q, xk, TN, preferred_element_type=F32) * 0.25 + 1.0
            weight = jnp.where(inside, dots * dots, 0.0).astype(BF16)
            both.append(jnp.dot(weight, vals, preferred_element_type=F32))
        tot[p] = jnp.where(left, both[0], both[1])
    phq[...] = (features(xq) * table[4:5, :]).astype(BF16)

    factor = math.log2(math.e) / math.sqrt(HEAD_DIM)
    own_docs = plane_docs[y]
    for k in range(8):
        d2[:, (8 + k) * 128 : (9 + k) * 128] = own_docs[k : k + 1]

    def doc_span(slot, count):
        return d2[:, pl.ds(pl.multiple_of(slot * 128, 128), count * 128)]

    def weigh(query, b, slot, count, low, high, start):
        docq = jnp.broadcast_to(query[1], (128, 128)).T[:, 0:1]
        keys = kv[b, pl.ds(slot, count), 0].reshape(count * 128, 128)
        scores = lax.dot_general(query[0], keys, NT, preferred_element_type=F32)
        off = lax.broadcasted_iota(jnp.int32, scores.shape, 1) - lax.broadcasted_iota(
            jnp.int32, scores.shape, 0
        )
        see = docq == doc_span(slot, count)
        if low is not None:
            see = see & (off > low)
        if high is not None:
            see = see & (off <= high)
        scores = jnp.where(see, scores, -1e30)
        peak = jnp.max(scores, axis=1, keepdims=True)
        if start is not None:
            peak = jnp.maximum(peak, start)
        prob = jnp.exp2((scores - peak) * factor)
        rowsum = jnp.sum(prob, axis=1, keepdims=True)
        values = kv[b, pl.ds(slot, count), 1].reshape(count * 128, 128)
        mixed = jnp.dot(prob.astype(BF16), values, preferred_element_type=F32)
        return peak, rowsum, mixed

    def attend(b, j, at):
        _, rowsum, mixed = weigh(
            (qb[at], doc_span(8 + j, 1)), b, j, BACK + 1, 0, BACK * 128, None
        )
        ob[at] = (mixed / rowsum).astype(BF16)

    def own_part(j, count):
        peak, rowsum, mixed = weigh(
            (qb[j], doc_span(8 + j, 1)), 0, 8, count, None, j * 128, None
        )
        peaks[j] = jnp.broadcast_to(peak, (128, 128))
        sums[j] = jnp.broadcast_to(rowsum, (128, 128))
        mixes[j] = mixed

    def last_part(j, first):
        before = peaks[j]
        peak, rowsum, mixed = weigh(
            (qb[j], doc_span(8 + j, 1)), 0, first, 8 - first, (j - first) * 128, None,
            before[:, 0:1],
        )
        fade = jnp.exp2((before - peak) * factor)
        ob[j] = ((mixed + mixes[j] * fade) / (rowsum + sums[j] * fade)).astype(BF16)

    for dx, dc in ORDER:
        s = frm(dx, dc)
        arrived(qb.at[s], rs_q.at[s])

    @pl.loop(4, 8)
    def _(j):
        own_part(j, 8)

    @pl.loop(0, 4)
    def _(j):
        own_part(j, 4)

    for k in (1, 2):
        arrived(wrecv.at[k - 1], rs_w.at[k])
    before = [wrecv[k].astype(F32) for k in range(2)]
    entering_doc = jnp.where(z >= 1, before[0][23:24, 127:128], -1.0)
    enter = jnp.where(z >= 1, before[0][:16], 0.0)
    same = jnp.where(z >= 2, before[1][23:24, 127:128], -2.0) == entering_doc
    enter = enter + jnp.where(same, before[1][:16], 0.0)
    fsend[0] = enter.astype(BF16)
    previous = entering_doc
    for k in range(1, PLANE_DEVS):
        fsend[k] = (running[k] + jnp.where(last[k - 1] == entering_doc, enter, 0.0)).astype(BF16)
        previous = jnp.where(me == k, last[k - 1], previous)

    for n, (place, outer_at, inner_at) in enumerate(others):
        remote(fsend.at[place], pf.at[me], ss_f.at[n], rs_f.at[me], outer_at, inner_at).start()
    pf[me] = fsend[me]
    docs_before = jnp.where(z >= 1, before[0][16:24], -1.0)
    docs_before = jnp.where(y >= 1, plane_docs[jnp.maximum(y - 1, 0)], docs_before)
    for k in range(8):
        d2[:, k * 128 : (k + 1) * 128] = docs_before[k : k + 1]

    def finish(j):
        @pl.when(j != i)
        def _():
            remote(ob.at[j], cols(wout, i), ss_o.at[j], rs_o.at[i], r, j).start()

        @pl.when(j == i)
        def _():
            pltpu.make_async_copy(ob.at[j], cols(wout, i), ss_o.at[j]).start()

    @pl.loop(0, 4)
    def _(step):
        arrived(kv.at[0, 7 - step], rs_prev.at[0, 7 - step])

    @pl.loop(0, 4)
    def _(step):
        last_part(7 - step, 4)
        finish(7 - step)

    @pl.loop(0, 4)
    def _(step):
        arrived(kv.at[0, 3 - step], rs_prev.at[0, 3 - step])

    @pl.loop(0, 4)
    def _(step):
        last_part(3 - step, 0)
        finish(3 - step)

    arrived(qb.at[9 - c], rs_q.at[9 - c])

    @pl.loop(0, 2 * x + 2)
    def _(s):
        @pl.when(s != i)
        def _():
            arrived(kv.at[1, 8 + s], rs_own.at[1, s])

    @pl.loop(2 * x, 8)
    def _(s):
        @pl.when(s != i)
        def _():
            arrived(kv.at[1, s], rs_prev.at[1, s])

    @pl.loop(0, 2)
    def _(step):
        core = lax.rem(1 - c + step, 2)
        attend(1, 2 * x + core, 8 + core)

        @pl.when(step == 0)
        def _():
            remote(ob.at[9 - c], cols(wout, 8 + c), ss_o.at[8], rs_o.at[8 + c], r, sib).start()

    pltpu.make_async_copy(ob.at[8 + c], cols(wout, 8 + c), ss_o.at[9]).start()

    for place, _, _ in others:
        arrived(pf.at[place], rs_f.at[place])

    carried = own_cols == previous
    for p in range(PAIRS):
        state = pf[p * GROUPS : (p + 1) * GROUPS].reshape(FEAT, 128)
        both = [
            jnp.dot(phq[:, h * 128 : h * 128 + FEAT], state, preferred_element_type=F32)
            for h in (2 * p, 2 * p + 1)
        ]
        total = tot[p] + jnp.where(carried, jnp.where(left, both[0], both[1]), 0.0)
        square = total * total
        one = jnp.sum(jnp.where(left, square, 0.0), axis=1, keepdims=True)
        two = jnp.sum(jnp.where(left, 0.0, square), axis=1, keepdims=True)
        mean = jnp.where(left, one, two) * (1.0 / BASED_DIM)
        scaled = total * lax.rsqrt(mean + 1e-5) * gain[p * 128 : (p + 1) * 128].reshape(1, 128)
        bout[:, p * 128 : (p + 1) * 128] = scaled.astype(BF16)

    @pl.loop(0, 8)
    def _(j):
        @pl.when(j != i)
        def _():
            arrived(cols(wout, j), rs_o.at[j])

    arrived(cols(wout, 9 - c), rs_o.at[9 - c])
    for src, ss in sent:
        arrived(src, ss)

    @pl.loop(0, PLANE_DEVS - 1)
    def _(n):
        arrived(ssend.at[0], ss_s.at[n])
        arrived(fsend.at[0], ss_f.at[n])

    for n, (dx, dc) in enumerate(FAR):

        @pl.when(x + dx < 4)
        def _():
            arrived(kv.at[1, 8 + i], ss_own.at[1, n + 1])

        @pl.when(x + dx >= 4)
        def _():
            arrived(cfw.at[0], ss_prev.at[1, n + 1])

    @pl.loop(0, 8)
    def _(j):
        arrived(ob.at[j], ss_o.at[j])

    arrived(ob.at[9 - c], ss_o.at[8])
    arrived(ob.at[8 + c], ss_o.at[9])


def hand_over(based, window, bout, wout, held_based, held_window, sems):
    loads = [
        pltpu.make_async_copy(window, held_window, sems.at[0]),
        pltpu.make_async_copy(based, held_based, sems.at[1]),
    ]
    stores = [
        pltpu.make_async_copy(held_window, wout, sems.at[2]),
        pltpu.make_async_copy(held_based, bout, sems.at[3]),
    ]
    for load in loads:
        load.start()
    for load, store in zip(loads, stores):
        load.wait()
        store.start()
    for store in stores:
        store.wait()


def body(outer, table, bq, bk, bv, gain, doc, wq, wk, wv):
    vmem = pl.BlockSpec(memory_space=pltpu.VMEM)
    anyw = pl.BlockSpec(memory_space=pl.ANY)
    dma = pltpu.SemaphoreType.DMA
    operands = (bq.T, bk.T, bv, gain, doc.reshape(1, -1), jnp.asarray(table), wq, wk, wv)
    parts = pl.pallas_call(
        functools.partial(kernel, outer),
        out_shape=(
            jax.ShapeDtypeStruct((ROWS, HEADS * BASED_DIM), BF16),
            jax.ShapeDtypeStruct((ROWS, WIN_HEADS * HEAD_DIM), BF16),
        ),
        in_specs=[anyw] * 9,
        out_specs=(vmem, anyw),
        scratch_shapes=[pltpu.VMEM(a.shape, a.dtype) for a in operands]
        + [
            pltpu.VMEM((10, 128, 128), BF16),
            pltpu.VMEM((10, 2, 128, 128), BF16),
            pltpu.VMEM((2, 16, 2, 128, 128), BF16),
            pltpu.VMEM((2, 2, 128, 128), BF16),
            pltpu.VMEM((10, 128, 128), BF16),
            pltpu.VMEM((10, 128, 128), BF16),
            pltpu.VMEM((1, 16 * 128), F32),
            pltpu.VMEM((PLANE_DEVS, 16, 128), BF16),
            pltpu.VMEM((PLANE_DEVS, 16, 128), BF16),
            pltpu.VMEM((PLANE_DEVS, 16, 128), F32),
            pltpu.VMEM((PLANE, 8, 128), F32),
            pltpu.VMEM((32, 128), BF16),
            pltpu.VMEM((2, 32, 128), BF16),
            pltpu.VMEM((PLANE_DEVS, 16, 128), BF16),
            pltpu.VMEM((PLANE_DEVS, 16, 128), BF16),
            pltpu.VMEM((PAIRS, 128, 128), F32),
            pltpu.VMEM((128, HEADS * 128), BF16),
            pltpu.VMEM((8, 128, 128), F32),
            pltpu.VMEM((8, 128, 128), F32),
            pltpu.VMEM((8, 128, 128), F32),
            dma((9,)), dma((2, 8)), dma((2, 8)), dma((2, 8)), dma((2, 8)),
            dma((10,)), dma((10,)), dma((10,)), dma((10,)), dma, dma,
            dma((PLANE_DEVS,)), dma((PLANE_DEVS,)), dma((3,)), dma((3,)),
            dma((PLANE_DEVS,)), dma((PLANE_DEVS,)),
        ],
        compiler_params=pltpu.CompilerParams(
            collective_id=0, has_side_effects=True, vmem_limit_bytes=60 << 20
        ),
        name="hybrid_attention",
    )(*operands)
    return pl.pallas_call(
        hand_over,
        out_shape=tuple(jax.ShapeDtypeStruct(a.shape, a.dtype) for a in parts),
        in_specs=[anyw] * 2,
        out_specs=(anyw, anyw),
        scratch_shapes=[pltpu.VMEM(a.shape, a.dtype) for a in parts] + [dma((4,))],
        compiler_params=pltpu.CompilerParams(vmem_limit_bytes=60 << 20),
        name="results",
    )(*parts)


def solution(mesh):
    tokens = P(("outer", "inner"), None)
    return jax.shard_map(
        functools.partial(body, mesh.shape["outer"], feature_table()),
        mesh=mesh,
        in_specs=(tokens, tokens, tokens, P(), P(("outer", "inner")), tokens, tokens, tokens),
        out_specs=(tokens, tokens),
        check_vma=False,
    )
```

```python
import functools
import math

import jax
import jax.numpy as jnp
import numpy as np
from jax import lax
from jax.experimental import pallas as pl
from jax.experimental.pallas import tpu as pltpu
from jax.sharding import PartitionSpec as P

HEADS = 10
BASED_DIM = 64
HEAD_DIM = 128
QK_DIM = 11
WIN_HEADS = 10
ROWS = 128
BACK = 8
PLANE = 4
PAIRS = HEADS // 2
GROUP = 13
GROUPS = 6
FEAT = GROUPS * 16
PLANE_DEVS = 32
MESH = pl.DeviceIdType.MESH
ORDER = ((0, 1), (1, 0), (1, 1), (3, 0), (3, 1), (2, 0), (2, 1))
FAR = ORDER[1:]
NT = (((1,), (1,)), ((), ()))
TN = (((0,), (0,)), ((), ()))
F32 = jnp.float32
BF16 = jnp.bfloat16


def feature_table():
    table = np.zeros((8, HEADS * 128), np.float32)
    table[:2] = -1.0
    for head in range(HEADS):
        feature = 0
        for a in range(QK_DIM + 1):
            for b in range(a, QK_DIM + 1):
                at = head * 128 + feature // GROUP * 16 + feature % GROUP
                for row, entry in ((0, a), (1, b)):
                    if entry == 0:
                        table[row + 2, at] = 1.0
                    else:
                        table[row, at] = head * QK_DIM + entry - 1
                table[4, at] = 1.0 if a == b else 2.0
                feature += 1
    return table


def kernel(
    outer,
    bq_hbm, bk_hbm, bv_hbm, gain_hbm, doc_hbm, aux_hbm, wq_hbm, wk_hbm, wv_hbm,
    bout, wout,
    bq, bk, bv, gain, doc, aux, wq, wk, wv,
    sq, skv, kv, cfw, qb, ob, d2, ssend, srecv, running, plane_docs, wsend, wrecv, fsend, pf, tot, phq,
    peaks, sums, mixes,
    ld, rs_own, ss_own, rs_prev, ss_prev, rs_q, ss_q, rs_o, ss_o, rs_c, ss_c,
    rs_s, ss_s, rs_w, ss_w, rs_f, ss_f,
):
    r = lax.axis_index("outer")
    i = lax.axis_index("inner")
    x = i // 2
    c = i % 2
    z = r // PLANE
    y = r % PLANE
    me = y * 8 + i
    up = lax.rem(r + 1, outer)
    sib = x * 2 + (1 - c)

    def to(dx, dc):
        return lax.rem(x + dx, 4) * 2 + lax.rem(c + dc, 2)

    plane_rows = [lax.rem(y + k, PLANE) for k in range(PLANE)]
    plane_outer = [z * PLANE + k for k in plane_rows]
    plane_inner = [lax.rem(i + k, 8) for k in range(8)]
    others = [
        (plane_rows[n // 8] * 8 + plane_inner[n % 8], plane_outer[n // 8], plane_inner[n % 8])
        for n in range(1, PLANE_DEVS)
    ]

    def frm(dx, dc):
        return lax.rem(x + 4 - dx, 4) * 2 + lax.rem(c + dc, 2)

    def cols(ref, head):
        return ref.at[:, pl.ds(pl.multiple_of(head * HEAD_DIM, HEAD_DIM), HEAD_DIM)]

    def remote(src, dst, ss, rs, row, inner):
        return pltpu.make_async_remote_copy(
            src_ref=src, dst_ref=dst, send_sem=ss, recv_sem=rs,
            device_id=(row, inner), device_id_type=MESH,
        )

    def arrived(dst, rs):
        pltpu.make_async_copy(dst, dst, rs).wait()

    sent = []

    def send(src, dst, ss, rs, row, inner):
        remote(src, dst, ss, rs, row, inner).start()
        sent.append((src, ss))


    barrier = pltpu.get_barrier_semaphore()
    senders = [lax.rem(r + outer - 1, outer)]
    senders += [lax.rem(r + outer - k * PLANE, outer) for k in (2, 1)]
    for other in senders:
        pl.semaphore_signal(barrier, inc=1, device_id=(other, i), device_id_type=MESH)
    for _, row, inner in others[7:]:
        pl.semaphore_signal(barrier, inc=1, device_id=(row, inner), device_id_type=MESH)
    for dx, dc in ORDER:
        pl.semaphore_signal(barrier, inc=1, device_id=(r, to(dx, dc)), device_id_type=MESH)

    loads = [
        pltpu.make_async_copy(src, dst, ld.at[n])
        for n, (src, dst) in enumerate(
            (
                (doc_hbm, doc), (bk_hbm, bk), (aux_hbm, aux), (bv_hbm, bv),
                (wk_hbm, wk), (wv_hbm, wv), (wq_hbm, wq), (bq_hbm, bq), (gain_hbm, gain),
            )
        )
    ]
    for load in loads:
        load.start()


    for load in loads[:4]:
        load.wait()
    doc_row = doc[...].astype(F32)
    table = aux[...]
    place = lax.broadcasted_iota(jnp.int32, (QK_DIM * HEADS, HEADS * 128), 0).astype(F32)
    pick_a = jnp.where(place == table[0:1, :], 0.5, 0.0).astype(BF16)
    pick_b = jnp.where(place == table[1:2, :], 0.5, 0.0).astype(BF16)
    xk = bk[...]

    def features(proj):
        first = lax.dot_general(proj, pick_a, TN, preferred_element_type=F32) + table[2:3, :]
        second = lax.dot_general(proj, pick_b, TN, preferred_element_type=F32) + table[3:4, :]
        return first * second

    lane = lax.broadcasted_iota(jnp.int32, (128, 128), 1)
    row = lax.broadcasted_iota(jnp.int32, (128, 128), 0)
    left = lane < BASED_DIM
    own_rows = jnp.broadcast_to(doc_row, (128, 128))
    own_cols = own_rows.T
    keep = own_cols == doc_row[:, 127:128]
    fk = features(xk).astype(BF16)
    docs_tail = jnp.broadcast_to(doc_row, (16, 128))
    tail = lax.broadcasted_iota(jnp.int32, (16, 128), 0) >= GROUP
    for p in range(PAIRS):
        vals = bv[:, p * 128 : (p + 1) * 128]
        kept = jnp.where(keep, vals.astype(F32), 0.0).astype(BF16)
        both = [
            lax.dot_general(
                fk[:, h * 128 : (h + 1) * 128], kept, TN, preferred_element_type=F32
            )
            for h in (2 * p, 2 * p + 1)
        ]
        state = jnp.where(left, both[0], both[1])
        for q in range(GROUPS):
            ssend[p * GROUPS + q] = jnp.where(
                tail, docs_tail, state[q * 16 : (q + 1) * 16]
            ).astype(BF16)
    for q in range(PAIRS * GROUPS, PLANE_DEVS):
        ssend[q] = docs_tail.astype(BF16)
    srecv[me] = ssend[me]

    for load in loads[4:6]:
        load.wait()
    for h in range(WIN_HEADS):
        skv[h, 0] = wk[:, h * 128 : (h + 1) * 128]
        skv[h, 1] = wv[:, h * 128 : (h + 1) * 128]

    pl.semaphore_wait(barrier, PLANE_DEVS - 1 + len(senders))

    for n, (place, outer_at, inner_at) in enumerate(others):
        remote(ssend.at[place], srecv.at[me], ss_s.at[n], rs_s.at[me], outer_at, inner_at).start()
    send(skv.at[8:10], cfw, ss_c, rs_c, up, i)
    send(skv.at[i], kv.at[0, i], ss_prev.at[0, i], rs_prev.at[0, i], up, i)

    def send_kv(steps):
        for n in steps:
            d = to(*ORDER[n])
            send(skv.at[d], kv.at[0, 8 + i], ss_own.at[0, n], rs_own.at[0, i], r, d)

    def pass_on(steps):
        for n in steps:
            s = frm(*ORDER[n])
            arrived(kv.at[0, 8 + s], rs_own.at[0, s])
            send(kv.at[0, 8 + s], kv.at[0, s], ss_prev.at[0, s], rs_prev.at[0, s], up, i)

    send_kv(range(5))
    for load in loads[6:]:
        load.wait()
    for h in range(WIN_HEADS):
        sq[h] = wq[:, h * 128 : (h + 1) * 128]
    send(sq.at[9 - c], qb.at[8 + c], ss_q.at[7], rs_q.at[8 + c], r, sib)
    send(skv.at[9 - c], kv.at[1, 8 + i], ss_own.at[1, 0], rs_own.at[1, i], r, sib)
    kv[0, 8 + i] = skv[i]
    kv[1, 8 + i] = skv[8 + c]
    qb[i] = sq[i]
    qb[8 + c] = sq[8 + c]

    pass_on(range(1))

    send_kv(range(5, 7))
    arrived(cfw, rs_c)
    kv[1, i] = cfw[c]
    send(cfw.at[1 - c], kv.at[1, i], ss_prev.at[1, 0], rs_prev.at[1, i], r, sib)
    pass_on(range(1, 5))
    for n, (dx, dc) in enumerate(ORDER):
        d = to(dx, dc)
        send(sq.at[d], qb.at[i], ss_q.at[n], rs_q.at[i], r, d)

    pass_on(range(5, 7))
    for place, _, _ in others:
        arrived(srecv.at[place], rs_s.at[place])

    messages = [srecv[k].astype(F32) for k in range(PLANE_DEVS)]
    last = [message[GROUP : GROUP + 1, 127:128] for message in messages]
    acc = messages[0]
    for k in range(1, PLANE_DEVS):
        running[k] = acc
        acc = messages[k] + jnp.where(last[k] == last[k - 1], acc, 0.0)
    sub = lax.broadcasted_iota(jnp.int32, (8, 128), 0)
    for k in range(PLANE):
        docs = jnp.zeros((8, 128), F32)
        for m in range(8):
            docs = jnp.where(sub == m, messages[k * 8 + m][GROUP : GROUP + 1, :], docs)
        plane_docs[k] = docs
    wsend[:16, :] = acc.astype(BF16)
    wsend[16:, :] = jnp.concatenate([docs, docs], axis=0).astype(BF16)
    for k in (1, 2):
        send(wsend, wrecv.at[k - 1], ss_w.at[k], rs_w.at[k], lax.rem(r + k * PLANE, outer), i)

    for n, (dx, dc) in enumerate(FAR):
        h = lax.rem(c + dc, 2)
        d = to(dx, dc)

        @pl.when(x + dx < 4)
        def _():
            remote(
                skv.at[8 + h], kv.at[1, 8 + i], ss_own.at[1, n + 1], rs_own.at[1, i], r, d
            ).start()

        @pl.when(x + dx >= 4)
        def _():
            remote(
                cfw.at[h], kv.at[1, i], ss_prev.at[1, n + 1], rs_prev.at[1, i], r, d
            ).start()


    xq = bq[...]
    inside = (own_cols == own_rows) & (lane <= row)
    lane_q = lax.broadcasted_iota(jnp.int32, (QK_DIM * HEADS, 128), 0)
    for p in range(PAIRS):
        vals = bv[:, p * 128 : (p + 1) * 128]
        both = []
        for h in (2 * p, 2 * p + 1):
            mine = (lane_q >= h * QK_DIM) & (lane_q < (h + 1) * QK_DIM)
            part_q = jnp.where(mine, xq.astype(F32), 0.0).astype(BF16)
            dots = lax.dot_general(part_q, xk, TN, preferred_element_type=F32) * 0.25 + 1.0
            weight = jnp.where(inside, dots * dots, 0.0).astype(BF16)
            both.append(jnp.dot(weight, vals, preferred_element_type=F32))
        tot[p] = jnp.where(left, both[0], both[1])
    phq[...] = (features(xq) * table[4:5, :]).astype(BF16)

    factor = math.log2(math.e) / math.sqrt(HEAD_DIM)
    own_docs = plane_docs[y]
    for k in range(8):
        d2[:, (8 + k) * 128 : (9 + k) * 128] = own_docs[k : k + 1]

    def doc_span(slot, count):
        return d2[:, pl.ds(pl.multiple_of(slot * 128, 128), count * 128)]

    def weigh(query, b, slot, count, low, high, start):
        docq = jnp.broadcast_to(query[1], (128, 128)).T[:, 0:1]
        keys = kv[b, pl.ds(slot, count), 0].reshape(count * 128, 128)
        scores = lax.dot_general(query[0], keys, NT, preferred_element_type=F32)
        off = lax.broadcasted_iota(jnp.int32, scores.shape, 1) - lax.broadcasted_iota(
            jnp.int32, scores.shape, 0
        )
        see = docq == doc_span(slot, count)
        if low is not None:
            see = see & (off > low)
        if high is not None:
            see = see & (off <= high)
        scores = jnp.where(see, scores, -1e30)
        peak = jnp.max(scores, axis=1, keepdims=True)
        if start is not None:
            peak = jnp.maximum(peak, start)
        prob = jnp.exp2((scores - peak) * factor)
        rowsum = jnp.sum(prob, axis=1, keepdims=True)
        values = kv[b, pl.ds(slot, count), 1].reshape(count * 128, 128)
        mixed = jnp.dot(prob.astype(BF16), values, preferred_element_type=F32)
        return peak, rowsum, mixed

    def attend(b, j, at):
        _, rowsum, mixed = weigh(
            (qb[at], doc_span(8 + j, 1)), b, j, BACK + 1, 0, BACK * 128, None
        )
        ob[at] = (mixed / rowsum).astype(BF16)

    def own_part(j, count):
        peak, rowsum, mixed = weigh(
            (qb[j], doc_span(8 + j, 1)), 0, 8, count, None, j * 128, None
        )
        peaks[j] = jnp.broadcast_to(peak, (128, 128))
        sums[j] = jnp.broadcast_to(rowsum, (128, 128))
        mixes[j] = mixed

    def last_part(j, first):
        before = peaks[j]
        peak, rowsum, mixed = weigh(
            (qb[j], doc_span(8 + j, 1)), 0, first, 8 - first, (j - first) * 128, None,
            before[:, 0:1],
        )
        fade = jnp.exp2((before - peak) * factor)
        ob[j] = ((mixed + mixes[j] * fade) / (rowsum + sums[j] * fade)).astype(BF16)

    for dx, dc in ORDER:
        s = frm(dx, dc)
        arrived(qb.at[s], rs_q.at[s])

    @pl.loop(4, 8)
    def _(j):
        own_part(j, 8)

    @pl.loop(0, 4)
    def _(j):
        own_part(j, 4)

    for k in (1, 2):
        arrived(wrecv.at[k - 1], rs_w.at[k])
    before = [wrecv[k].astype(F32) for k in range(2)]
    entering_doc = jnp.where(z >= 1, before[0][23:24, 127:128], -1.0)
    enter = jnp.where(z >= 1, before[0][:16], 0.0)
    same = jnp.where(z >= 2, before[1][23:24, 127:128], -2.0) == entering_doc
    enter = enter + jnp.where(same, before[1][:16], 0.0)
    fsend[0] = enter.astype(BF16)
    previous = entering_doc
    for k in range(1, PLANE_DEVS):
        fsend[k] = (running[k] + jnp.where(last[k - 1] == entering_doc, enter, 0.0)).astype(BF16)
        previous = jnp.where(me == k, last[k - 1], previous)

    for n, (place, outer_at, inner_at) in enumerate(others):
        remote(fsend.at[place], pf.at[me], ss_f.at[n], rs_f.at[me], outer_at, inner_at).start()
    pf[me] = fsend[me]
    docs_before = jnp.where(z >= 1, before[0][16:24], -1.0)
    docs_before = jnp.where(y >= 1, plane_docs[jnp.maximum(y - 1, 0)], docs_before)
    for k in range(8):
        d2[:, k * 128 : (k + 1) * 128] = docs_before[k : k + 1]

    def finish(j):
        @pl.when(j != i)
        def _():
            remote(ob.at[j], cols(wout, i), ss_o.at[j], rs_o.at[i], r, j).start()

        @pl.when(j == i)
        def _():
            pltpu.make_async_copy(ob.at[j], cols(wout, i), ss_o.at[j]).start()

    def finish_pair(first):
        for slot in (first + 1, first):
            arrived(kv.at[0, slot], rs_prev.at[0, slot])

        @pl.loop(0, 2)
        def _(step):
            last_part(first + 1 - step, first)
            finish(first + 1 - step)

    for first in (6, 4, 2, 0):
        finish_pair(first)

    arrived(qb.at[9 - c], rs_q.at[9 - c])

    @pl.loop(0, 2 * x + 2)
    def _(s):
        @pl.when(s != i)
        def _():
            arrived(kv.at[1, 8 + s], rs_own.at[1, s])

    @pl.loop(2 * x, 8)
    def _(s):
        @pl.when(s != i)
        def _():
            arrived(kv.at[1, s], rs_prev.at[1, s])

    @pl.loop(0, 2)
    def _(step):
        core = lax.rem(1 - c + step, 2)
        attend(1, 2 * x + core, 8 + core)

        @pl.when(step == 0)
        def _():
            remote(ob.at[9 - c], cols(wout, 8 + c), ss_o.at[8], rs_o.at[8 + c], r, sib).start()

    pltpu.make_async_copy(ob.at[8 + c], cols(wout, 8 + c), ss_o.at[9]).start()

    for place, _, _ in others:
        arrived(pf.at[place], rs_f.at[place])

    carried = own_cols == previous
    for p in range(PAIRS):
        state = pf[p * GROUPS : (p + 1) * GROUPS].reshape(FEAT, 128)
        both = [
            jnp.dot(phq[:, h * 128 : h * 128 + FEAT], state, preferred_element_type=F32)
            for h in (2 * p, 2 * p + 1)
        ]
        total = tot[p] + jnp.where(carried, jnp.where(left, both[0], both[1]), 0.0)
        square = total * total
        one = jnp.sum(jnp.where(left, square, 0.0), axis=1, keepdims=True)
        two = jnp.sum(jnp.where(left, 0.0, square), axis=1, keepdims=True)
        mean = jnp.where(left, one, two) * (1.0 / BASED_DIM)
        scaled = total * lax.rsqrt(mean + 1e-5) * gain[p * 128 : (p + 1) * 128].reshape(1, 128)
        bout[:, p * 128 : (p + 1) * 128] = scaled.astype(BF16)

    @pl.loop(0, 8)
    def _(j):
        @pl.when(j != i)
        def _():
            arrived(cols(wout, j), rs_o.at[j])

    arrived(cols(wout, 9 - c), rs_o.at[9 - c])
    for src, ss in sent:
        arrived(src, ss)

    @pl.loop(0, PLANE_DEVS - 1)
    def _(n):
        arrived(ssend.at[0], ss_s.at[n])
        arrived(fsend.at[0], ss_f.at[n])

    for n, (dx, dc) in enumerate(FAR):

        @pl.when(x + dx < 4)
        def _():
            arrived(kv.at[1, 8 + i], ss_own.at[1, n + 1])

        @pl.when(x + dx >= 4)
        def _():
            arrived(cfw.at[0], ss_prev.at[1, n + 1])

    @pl.loop(0, 8)
    def _(j):
        arrived(ob.at[j], ss_o.at[j])

    arrived(ob.at[9 - c], ss_o.at[8])
    arrived(ob.at[8 + c], ss_o.at[9])


def hand_over(based, window, bout, wout, held_based, held_window, sems):
    loads = [
        pltpu.make_async_copy(window, held_window, sems.at[0]),
        pltpu.make_async_copy(based, held_based, sems.at[1]),
    ]
    stores = [
        pltpu.make_async_copy(held_window, wout, sems.at[2]),
        pltpu.make_async_copy(held_based, bout, sems.at[3]),
    ]
    for load in loads:
        load.start()
    for load, store in zip(loads, stores):
        load.wait()
        store.start()
    for store in stores:
        store.wait()


def body(outer, table, bq, bk, bv, gain, doc, wq, wk, wv):
    vmem = pl.BlockSpec(memory_space=pltpu.VMEM)
    anyw = pl.BlockSpec(memory_space=pl.ANY)
    dma = pltpu.SemaphoreType.DMA
    operands = (bq.T, bk.T, bv, gain, doc.reshape(1, -1), jnp.asarray(table), wq, wk, wv)
    parts = pl.pallas_call(
        functools.partial(kernel, outer),
        out_shape=(
            jax.ShapeDtypeStruct((ROWS, HEADS * BASED_DIM), BF16),
            jax.ShapeDtypeStruct((ROWS, WIN_HEADS * HEAD_DIM), BF16),
        ),
        in_specs=[anyw] * 9,
        out_specs=(vmem, anyw),
        scratch_shapes=[pltpu.VMEM(a.shape, a.dtype) for a in operands]
        + [
            pltpu.VMEM((10, 128, 128), BF16),
            pltpu.VMEM((10, 2, 128, 128), BF16),
            pltpu.VMEM((2, 16, 2, 128, 128), BF16),
            pltpu.VMEM((2, 2, 128, 128), BF16),
            pltpu.VMEM((10, 128, 128), BF16),
            pltpu.VMEM((10, 128, 128), BF16),
            pltpu.VMEM((1, 16 * 128), F32),
            pltpu.VMEM((PLANE_DEVS, 16, 128), BF16),
            pltpu.VMEM((PLANE_DEVS, 16, 128), BF16),
            pltpu.VMEM((PLANE_DEVS, 16, 128), F32),
            pltpu.VMEM((PLANE, 8, 128), F32),
            pltpu.VMEM((32, 128), BF16),
            pltpu.VMEM((2, 32, 128), BF16),
            pltpu.VMEM((PLANE_DEVS, 16, 128), BF16),
            pltpu.VMEM((PLANE_DEVS, 16, 128), BF16),
            pltpu.VMEM((PAIRS, 128, 128), F32),
            pltpu.VMEM((128, HEADS * 128), BF16),
            pltpu.VMEM((8, 128, 128), F32),
            pltpu.VMEM((8, 128, 128), F32),
            pltpu.VMEM((8, 128, 128), F32),
            dma((9,)), dma((2, 8)), dma((2, 8)), dma((2, 8)), dma((2, 8)),
            dma((10,)), dma((10,)), dma((10,)), dma((10,)), dma, dma,
            dma((PLANE_DEVS,)), dma((PLANE_DEVS,)), dma((3,)), dma((3,)),
            dma((PLANE_DEVS,)), dma((PLANE_DEVS,)),
        ],
        compiler_params=pltpu.CompilerParams(
            collective_id=0, has_side_effects=True, vmem_limit_bytes=60 << 20
        ),
        name="hybrid_attention",
    )(*operands)
    return pl.pallas_call(
        hand_over,
        out_shape=tuple(jax.ShapeDtypeStruct(a.shape, a.dtype) for a in parts),
        in_specs=[anyw] * 2,
        out_specs=(anyw, anyw),
        scratch_shapes=[pltpu.VMEM(a.shape, a.dtype) for a in parts] + [dma((4,))],
        compiler_params=pltpu.CompilerParams(vmem_limit_bytes=60 << 20),
        name="results",
    )(*parts)


def solution(mesh):
    tokens = P(("outer", "inner"), None)
    return jax.shard_map(
        functools.partial(body, mesh.shape["outer"], feature_table()),
        mesh=mesh,
        in_specs=(tokens, tokens, tokens, P(), P(("outer", "inner")), tokens, tokens, tokens),
        out_specs=(tokens, tokens),
        check_vma=False,
    )
```
